512 devices in a mesh: seq: 64 (over x, z), tp: 8 (over y, core).
Axes of the slice: x: 4, y: 4, z: 16, core: 2. Of those that a mesh axis runs over, the one named last changes fastest.
Arguments:
- x_in: bfloat16 [32768, 5120], P('seq', 'tp'), may hold values from -17 to 17
- bc_in: bfloat16 [32768, 256], P('seq'), may hold values from -17 to 17
- z_gate: bfloat16 [32768, 5120], P('seq', 'tp'), may hold values from -6 to 6
- dt_in: bfloat16 [32768, 80], P('seq', 'tp'), may hold values from -3 to 3
- conv_x: float32 [4, 5120], P(None, 'tp'), may hold values from -3.05 to 3.05
- conv_bc: float32 [4, 256], replicated, may hold values from -3.05 to 3.05
- dt_bias: float32 [80], P('tp'), may hold values from -9 to 0
- a_log: float32 [80], P('tp'), may hold values from -7 to 0
- d_skip: float32 [80], P('tp'), may hold values from 0.5 to 1.5
- norm_gain: float32 [5120], P('tp'), may hold values from 0.5 to 1.5
- out_weight: bfloat16 [5120, 2560], P('tp', 'seq'), may hold values from -0.078125 to 0.078125
Outputs:
- mixed: bfloat16 [32768, 2560], P('seq', 'tp')
The draws below stay inside these ranges and needn't reach their ends.
All inputs are finite; a program needn't handle non-finite values.
Results may differ from the reference program's by a relative error of at most 0.017.
Values may be sent and summed in bfloat16 or wider, within the bound.
No kernel may reach another device: no remote copies, remote signals or barrier semaphores. Data moves between devices by JAX's collectives and lax.ppermute only.
A program may use at most 128 MiB of HBM per device.

```python
import jax
import jax.numpy as jnp
from jax import lax

D = 2560
HEADS = 80
HEADDIM = 64
STATE = 128
CONV = 4
GROUP = 256
INNER = 5120
TOKENS = 32768
N_TP = 8


pre_centre = -1.13


pre_spread = 1.5


def head_scales(key, slow_share):
    flags = jax.random.uniform(jax.random.fold_in(key, 11), (HEADS,)) < slow_share
    slow_span = TOKENS * jnp.exp(jax.random.uniform(jax.random.fold_in(key, 12), (HEADS,), jnp.float32, jnp.log(0.5), jnp.log(2.0)))
    fast_span = jnp.exp(jax.random.uniform(jax.random.fold_in(key, 13), (HEADS,), jnp.float32, jnp.log(25.0), jnp.log(50.0)))
    span = jnp.where(flags, slow_span, fast_span)
    step_size = jnp.where(flags, 1.2 / jnp.sqrt(span), 1.0 / (3.6 * jnp.sqrt(span)))
    return (span, step_size)


def tap_design(key, marker, columns):
    base = jax.random.fold_in(key, marker)
    leading = jnp.clip(0.3 * jax.random.normal(jax.random.fold_in(base, 1), (CONV - 1, columns), jnp.float32), -0.6, 0.6)
    magnitude = jax.random.uniform(jax.random.fold_in(base, 2), (columns,), jnp.float32, 0.8, 1.25)
    polarity = jnp.where(jax.random.bernoulli(jax.random.fold_in(base, 3), 0.5, (columns,)), 1.0, -1.0)
    tap_total = polarity * magnitude
    last_tap = tap_total - jnp.sum(leading, axis=0)
    taps = jnp.concatenate([leading, last_tap[None, :]], axis=0)
    tap_norm = jnp.sqrt(jnp.sum(taps * taps, axis=0))
    return (taps, tap_total, tap_norm)


def channel_values(key, taps_total, tap_norm, rows, columns):
    offset = pre_centre / taps_total
    width = pre_spread / tap_norm
    jitter = jnp.clip(jax.random.normal(key, (rows, columns), jnp.float32), -4.0, 4.0)
    return offset[None, :] + width[None, :] * jitter


def draw_conv_x(key, part):
    taps, tap_total, tap_norm = tap_design(key, 31, INNER)
    return taps.astype(jnp.float32)


def draw_x_in(key, part):
    taps, tap_total, tap_norm = tap_design(key, 31, INNER)
    key = jax.random.fold_in(key, 4)
    return channel_values(key, tap_total, tap_norm, TOKENS, INNER).astype(jnp.bfloat16)


def draw_conv_bc(key, part):
    taps, tap_total, tap_norm = tap_design(key, 32, 2 * STATE)
    return taps.astype(jnp.float32)


def draw_bc_in(key, part):
    taps, tap_total, tap_norm = tap_design(key, 32, 2 * STATE)
    key = jax.random.fold_in(key, 6)
    return channel_values(key, tap_total, tap_norm, TOKENS, 2 * STATE).astype(jnp.bfloat16)


def draw_dt_bias(key, part):
    span, step_size = head_scales(key, 0.5)
    return jnp.log(jnp.expm1(step_size)).astype(jnp.float32)


def draw_a_log(key, part):
    span, step_size = head_scales(key, 0.5)
    return (-jnp.log(span) - jnp.log(step_size)).astype(jnp.float32)


def shard_levels(rng, shape, shards, least, high):
    level, own = 1.0, jax.random.fold_in(rng, 6)
    for dim, shards_of in shards:
        heights = jnp.exp(jax.random.uniform(jax.random.fold_in(own, dim), (shards_of,), jnp.float32, least / len(shards), high / len(shards)))
        level = level * jnp.repeat(heights, shape[dim] // shards_of).reshape([-1 if axis == dim else 1 for axis in range(len(shape))])
    return level


def scatter_about(own_key, shape, scale, bound, shards=(), held_as=jnp.bfloat16):
    values = scale * jax.random.normal(own_key, shape, jnp.float32)
    if shards:
        values = values * shard_levels(own_key, shape, shards, -0.22, 0.18)
    return jnp.clip(values, -bound, bound).astype(held_as)


def setup_inputs(seed: int = 0) -> dict:
    key_list = jax.random.split(jax.random.key(seed), 12)
    x_in = draw_x_in(jax.random.fold_in(key_list[11], 71), 0)
    bc_in = draw_bc_in(jax.random.fold_in(key_list[11], 71), 0)
    z_gate = scatter_about(key_list[2], (TOKENS, INNER), 1.0, 6.0, ((0, 64), (1, 8)))
    dt_in = scatter_about(key_list[3], (TOKENS, HEADS), 0.5, 3.0, ((0, 64), (1, 8)))
    conv_x = draw_conv_x(jax.random.fold_in(key_list[11], 71), 0)
    conv_bc = draw_conv_bc(jax.random.fold_in(key_list[11], 71), 0)
    dt_bias = draw_dt_bias(jax.random.fold_in(key_list[11], 71), 0)
    a_log = draw_a_log(jax.random.fold_in(key_list[11], 71), 0)
    d_skip = jnp.clip(0.5 + 1.0 * jax.random.uniform(key_list[8], (HEADS,), jnp.float32) ** shard_levels(key_list[8], (HEADS,), ((0, 8),), -0.2, 0.2), 0.5, 1.5)
    norm_gain = jnp.clip(1.0 + 0.1 * jax.random.normal(key_list[9], (INNER,), jnp.float32), 0.5, 1.5)
    out_weight = scatter_about(key_list[10], (INNER, D), INNER ** -0.5, 0.078125, ((0, 8), (1, 64)))
    return {"x_in": x_in, "bc_in": bc_in, "z_gate": z_gate, "dt_in": dt_in, "conv_x": conv_x, "conv_bc": conv_bc, "dt_bias": dt_bias, "a_log": a_log, "d_skip": d_skip, "norm_gain": norm_gain, "out_weight": out_weight}


EPSILON = 1e-05
HIGH = lax.Precision.HIGHEST

def causal_mix(values, weights):
    length = values.shape[0]
    padded = jnp.pad(values.astype(jnp.float32), ((CONV - 1, 0), (0, 0)))
    total = jnp.zeros(values.shape, jnp.float32)
    for offset in range(CONV):
        total = total + weights[offset][None, :] * padded[offset:offset + length]
    return jax.nn.silu(total).astype(jnp.bfloat16)

def block_step(carry, inputs):
    x_block, b_block, c_block, step_block, rate_block = inputs
    cumul = jnp.cumsum(rate_block, axis=0)
    causal = jnp.arange(GROUP)[:, None] >= jnp.arange(GROUP)[None, :]
    spread = cumul[:, None, :] - cumul[None, :, :]
    decays = jnp.where(causal[:, :, None], jnp.exp(jnp.where(causal[:, :, None], spread, 0.0)), 0.0)
    inner_cb = jnp.dot(c_block, b_block.T, precision=HIGH)
    mix_weights = inner_cb[:, :, None] * decays * step_block[None, :, :]
    result = jnp.einsum('tsh,shp->thp', mix_weights, x_block, precision=HIGH)
    result = result + jnp.exp(cumul)[:, :, None] * jnp.einsum('tn,hpn->thp', c_block, carry, precision=HIGH)
    tail = jnp.exp(cumul[-1][None, :] - cumul) * step_block
    fresh = jnp.einsum('sh,shp,sn->hpn', tail, x_block, b_block, precision=HIGH)
    carry = jnp.exp(cumul[-1])[:, None, None] * carry + fresh
    return (carry, result)

def reference(x_in, bc_in, z_gate, dt_in, conv_x, conv_bc, dt_bias, a_log, d_skip, norm_gain, out_weight):
    xc = causal_mix(x_in, conv_x)
    bcc = causal_mix(bc_in, conv_bc)
    step = jax.nn.softplus(dt_in.astype(jnp.float32) + dt_bias[None, :])
    rate = -jnp.exp(a_log)[None, :] * step
    blocks = TOKENS // GROUP
    x_blocks = xc.astype(jnp.float32).reshape(blocks, GROUP, HEADS, HEADDIM)
    b_blocks = bcc[:, :STATE].astype(jnp.float32).reshape(blocks, GROUP, STATE)
    c_blocks = bcc[:, STATE:].astype(jnp.float32).reshape(blocks, GROUP, STATE)
    start = jnp.zeros((HEADS, HEADDIM, STATE), jnp.float32)
    final, outputs = lax.scan(block_step, start, (x_blocks, b_blocks, c_blocks, step.reshape(blocks, GROUP, HEADS), rate.reshape(blocks, GROUP, HEADS)))
    result = outputs.reshape(TOKENS, HEADS, HEADDIM) + d_skip[None, :, None] * xc.astype(jnp.float32).reshape(TOKENS, HEADS, HEADDIM)
    gated = result.reshape(TOKENS, INNER) * jax.nn.silu(z_gate.astype(jnp.float32))
    mean_square = lax.optimization_barrier(jnp.mean(gated * gated, axis=1, keepdims=True))
    normed = (gated * lax.rsqrt(mean_square + EPSILON) * norm_gain[None, :]).astype(jnp.bfloat16)
    width = INNER // N_TP
    total = jnp.zeros((TOKENS, D), jnp.float32)
    for block in range(N_TP):
        piece = jnp.dot(normed[:, block * width:(block + 1) * width], out_weight[block * width:(block + 1) * width], preferred_element_type=jnp.float32)
        total = total + piece.astype(jnp.bfloat16).astype(jnp.float32)
    return total.astype(jnp.bfloat16)
```

```python
import jax
import jax.numpy as jnp
from jax import lax
from jax.experimental import pallas as pl
from jax.experimental.pallas import tpu as pltpu
from jax.sharding import PartitionSpec as P

CHANNELS = 5120
HEADDIM = 64
STATE = 128
CONV = 4
CHUNK = 128
LANES = 128
RIM = 16
PAD_HEADS = 16
PIECE = 16
EPSILON = 1e-05
HIGH = lax.Precision.HIGHEST
F32 = jnp.float32
BF16 = jnp.bfloat16
MASKED = -1e30
INTERPRET = False

NT = (((1,), (1,)), ((), ()))
TN = (((0,), (0,)), ((), ()))
NN = (((1,), (0,)), ((), ()))


def dot(a, b, dims=NN, precision=None):
    return lax.dot_general(a, b, dims, precision=precision, preferred_element_type=F32)


def call(body, outs, flops, *args, scratch=()):
    moved = sum(a.size * a.dtype.itemsize for a in args) + sum(
        o.size * o.dtype.itemsize for o in outs
    )
    return pl.pallas_call(
        body,
        out_shape=outs,
        in_specs=[pl.BlockSpec(memory_space=pltpu.VMEM)] * len(args),
        out_specs=[pl.BlockSpec(memory_space=pltpu.VMEM)] * len(outs),
        scratch_shapes=list(scratch),
        compiler_params=pltpu.CompilerParams(vmem_limit_bytes=40 * 2**20),
        cost_estimate=pl.CostEstimate(flops=flops, bytes_accessed=moved, transcendentals=0),
        interpret=INTERPRET,
    )(*args)


def silu(v):
    half = 0.5 * v
    return half + half * jnp.tanh(half)


def split(v):
    hi = v.astype(BF16)
    return hi, (v - hi.astype(F32)).astype(BF16)


def iota(shape, dim):
    return lax.broadcasted_iota(jnp.int32, shape, dim)


def as_column(row):
    heads = row.shape[1]
    same = iota((PAD_HEADS, heads), 0) == iota((PAD_HEADS, heads), 1)
    return jnp.sum(jnp.where(same, row, 0.0), axis=1, keepdims=True)


def head_spread(width, dtype):
    return (iota((PAD_HEADS, width), 1) // HEADDIM == iota((PAD_HEADS, width), 0)).astype(dtype)


def spread_tokens(per_head, spread2):
    hi, lo = split(per_head)
    return dot(jnp.concatenate([hi, lo], axis=0), spread2, TN)


def spread_row(column, spread_f32):
    return jnp.sum(spread_f32 * column, axis=0, keepdims=True)


def conv_silu(rim, value, taps_ref, scratch, out_ref):
    rows, width = value.shape
    scratch[0:8, :] = rim[RIM - 8 :, :].astype(F32)
    scratch[8 : 8 + rows, :] = value[...].astype(F32)
    first = 8 - (CONV - 1)
    for at in range(0, rows, CHUNK):
        total = taps_ref[0:1, :] * scratch[first + at : first + at + CHUNK, :]
        for k in range(1, CONV):
            total += taps_ref[k : k + 1, :] * scratch[first + at + k : first + at + k + CHUNK, :]
        out_ref[at : at + CHUNK, :] = silu(total).astype(BF16)


def front_kernel(
    x_ref, bc_ref, rim_ref, dt_ref, tap_x_ref, tap_bc_ref, bias_ref, alog_ref,
    xc_ref, bcc_ref, cum_ref, logstep_ref, piece_ref, x_scr, bc_scr, piece_scr,
):
    tokens, width = x_ref.shape
    heads = dt_ref.shape[1]
    rim = rim_ref[...]
    conv_silu(rim[:, :width], x_ref, tap_x_ref, x_scr, xc_ref)
    conv_silu(rim[:, width:], bc_ref, tap_bc_ref, bc_scr, bcc_ref)

    eye = (iota((PAD_HEADS, heads), 0) == iota((PAD_HEADS, heads), 1)).astype(BF16)
    logits = dot(eye, dt_ref[...], NT) + as_column(bias_ref[...])
    small = jnp.exp(-jnp.abs(logits))
    series = small * (1.0 - small * (0.5 - small * (1.0 / 3.0 - small * 0.25)))
    step = jnp.maximum(logits, 0.0) + jnp.where(small < 0.015625, series, jnp.log(1.0 + small))
    logstep = jnp.log(step)
    rate = -jnp.exp(as_column(alog_ref[...])) * step

    upto = (iota((CHUNK, CHUNK), 0) <= iota((CHUNK, CHUNK), 1)).astype(F32)
    run = jnp.zeros((PAD_HEADS, 1), F32)
    sums = []
    for at in range(0, tokens, CHUNK):
        within = dot(rate[:, at : at + CHUNK], upto, precision=HIGH) + run
        run = within[:, CHUNK - 1 :]
        sums.append(within)
    cum = jnp.concatenate(sums, axis=1)
    cum_ref[...] = cum
    logstep_ref[...] = logstep

    spread = head_spread(width, BF16)
    spread2 = jnp.concatenate([spread, spread], axis=0)
    tail = spread_tokens(jnp.exp(run - cum + logstep), spread2)
    fed = (xc_ref[...].astype(F32) * tail).astype(BF16)
    state = dot(bcc_ref[:, :STATE], fed, TN)

    spread_f = head_spread(width, F32)
    hi, lo = split(run)
    even = iota((1, width), 1) % 2 == 0
    decay = jnp.where(
        even, spread_row(hi.astype(F32), spread_f), spread_row(lo.astype(F32), spread_f)
    )
    half = STATE // 2
    blocks = width // LANES
    for b in range(blocks):
        cols = slice(b * LANES, (b + 1) * LANES)
        piece_scr[pl.ds(b, half, PIECE), :] = state[:half, cols]
        piece_scr[pl.ds(blocks + b, half, PIECE), :] = state[half:, cols]
        piece_scr[pl.ds(2 * blocks + b, half, PIECE), :] = jnp.broadcast_to(
            decay[:, cols], (half, LANES)
        )
    piece_scr[pl.ds(3 * blocks, half, PIECE), :] = jnp.zeros((half, LANES), F32)
    piece_ref[...] = piece_scr[...].astype(BF16)


def local_kernel(
    xc_ref, bcc_ref, cum_ref, logstep_ref, z_ref, skip_ref, own_ref, reach_ref, held,
):
    tokens, width = xc_ref.shape
    spread = head_spread(width, BF16)
    spread2 = jnp.concatenate([spread, spread], axis=0)
    spread_f = head_spread(width, F32)
    skip = spread_row(as_column(skip_ref[...]), spread_f)
    causal = iota((CHUNK, CHUNK), 0) >= iota((CHUNK, CHUNK), 1)
    left = iota((CHUNK, LANES), 1) < HEADDIM
    held[...] = jnp.zeros_like(held)
    before = jnp.zeros((PAD_HEADS, 1), F32)
    for at in range(0, tokens, CHUNK):
        rows = slice(at, at + CHUNK)
        b_part, c_part = bcc_ref[rows, :STATE], bcc_ref[rows, STATE:]
        cum = cum_ref[:, rows]
        source = logstep_ref[:, rows] - cum
        cum_cols = cum.T
        last = cum[:, CHUNK - 1 :]
        cb = dot(c_part, b_part, NT)
        gate = silu(z_ref[rows, :].astype(F32))
        reach_ref[rows, :] = spread_tokens(jnp.exp(cum), spread2) * gate
        fresh = spread_tokens(jnp.exp(cum - before), spread2)
        carried = dot(c_part, held[...].astype(BF16)) * fresh
        for pair in range(width // LANES):
            cols = slice(pair * LANES, (pair + 1) * LANES)
            mixes = []
            for head in (2 * pair, 2 * pair + 1):
                power = cum_cols[:, head : head + 1] + source[head : head + 1, :]
                mixes.append((cb * jnp.exp(jnp.where(causal, power, MASKED))).astype(BF16))
            x_part = xc_ref[rows, cols]
            blank = jnp.zeros_like(x_part)
            x_two = jnp.concatenate(
                [jnp.where(left, x_part, blank), jnp.where(left, blank, x_part)], axis=0
            )
            y = dot(jnp.concatenate(mixes, axis=1), x_two) + carried[:, cols]
            y += skip[:, cols] * x_part.astype(F32)
            own_ref[rows, cols] = y * gate[:, cols]
        if at + CHUNK < tokens:
            tail = spread_tokens(jnp.exp(last + source), spread2)
            fed = (xc_ref[rows, :].astype(F32) * tail).astype(BF16)
            kept = spread_row(jnp.exp(last - before), spread_f)
            held[...] = held[...] * kept + dot(b_part, fed, TN)
            before = last


def scan_kernel(blocks, in_ref, out_ref, wide):
    count = in_ref.shape[0] // PIECE
    wide[...] = in_ref[...].astype(F32)
    even = iota((blocks, LANES), 1) % 2 == 0
    low = jnp.zeros((blocks, LANES), F32)
    high = jnp.zeros((blocks, LANES), F32)
    for place in range(count):
        at = place * PIECE
        part = wide[at : at + blocks, :]
        part_high = wide[at + blocks : at + 2 * blocks, :]
        wide_decay = wide[at + 2 * blocks : at + 3 * blocks, :]
        other = jnp.where(
            even, pltpu.roll(wide_decay, LANES - 1, 1), pltpu.roll(wide_decay, 1, 1)
        )
        kept = jnp.exp(wide_decay + other)
        wide[at : at + blocks, :] = low
        wide[at + blocks : at + 2 * blocks, :] = high
        low = kept * low + part
        high = kept * high + part_high
    out_ref[...] = wide[...].astype(BF16)


def back_kernel(
    own_ref, reach_ref, c_ref, piece_ref, w_ref, gain_ref, place_ref, out_ref, wide, state, gated,
):
    tokens, width = own_ref.shape
    blocks = width // LANES
    half = STATE // 2
    wide[...] = piece_ref[...].astype(F32)
    for b in range(blocks):
        cols = slice(b * LANES, (b + 1) * LANES)
        state[:half, cols] = wide[pl.ds(b, half, PIECE), :]
        state[half:, cols] = wide[pl.ds(blocks + b, half, PIECE), :]
    incoming = state[...].astype(BF16)
    ones = jnp.ones((16, 2 * width), BF16)
    totals = []
    for at in range(0, tokens, CHUNK):
        rows = slice(at, at + CHUNK)
        y = own_ref[rows, :] + reach_ref[rows, :] * dot(c_ref[rows, STATE:], incoming)
        gated[rows, :] = (y * gain_ref[...]).astype(BF16)
        hi, lo = split(y * y)
        totals.append(dot(ones, jnp.concatenate([hi, lo], axis=1), NT))
    hi, lo = split(jnp.concatenate(totals, axis=1))
    row = iota((16, tokens), 0)
    mine = 2 * place_ref[0, 0]
    zero = jnp.zeros((16, tokens), F32)
    squares = jnp.where(
        row == mine, hi.astype(F32), jnp.where(row == mine + 1, lo.astype(F32), zero)
    ).astype(BF16)
    targets = 8
    each = w_ref.shape[0] // targets
    for d in range(targets):
        to = d * (each + 16)
        out_ref[to : to + each, :] = dot(
            w_ref[d * each : (d + 1) * each, :], gated[...], NT
        ).astype(BF16)
        out_ref[to + each : to + each + 16, :] = squares


def scale_kernel(in_ref, out_ref):
    each = out_ref.shape[1]
    total = jnp.sum(in_ref[each:, :].astype(F32), axis=0, keepdims=True)
    scale = lax.rsqrt(total / CHANNELS + EPSILON)
    out_ref[...] = (in_ref[:each, :].astype(F32) * scale).T.astype(BF16)


def front(x_in, bc_in, rim, dt_in, conv_x, conv_bc, dt_bias, a_log):
    tokens, width = x_in.shape
    return call(
        front_kernel,
        [
            jax.ShapeDtypeStruct((tokens, width), BF16),
            jax.ShapeDtypeStruct((tokens, 2 * STATE), BF16),
            jax.ShapeDtypeStruct((PAD_HEADS, tokens), F32),
            jax.ShapeDtypeStruct((PAD_HEADS, tokens), F32),
            jax.ShapeDtypeStruct((STATE // 2 * PIECE, LANES), BF16),
        ],
        2 * tokens * width * STATE,
        x_in, bc_in, rim, dt_in, conv_x, conv_bc, dt_bias[None], a_log[None],
        scratch=(
            pltpu.VMEM((tokens + 8, width), F32),
            pltpu.VMEM((tokens + 8, 2 * STATE), F32),
            pltpu.VMEM((STATE // 2 * PIECE, LANES), F32),
        ),
    )


def local(xc, bcc, cum, logstep, z_gate, d_skip):
    tokens, width = xc.shape
    return call(
        local_kernel,
        [jax.ShapeDtypeStruct((tokens, width), F32)] * 2,
        6 * tokens * width * STATE,
        xc, bcc, cum, logstep, z_gate, d_skip[None],
        scratch=(pltpu.VMEM((STATE, width), F32),),
    )


def scan(pieces, width):
    def body(*refs):
        scan_kernel(width // LANES, *refs)

    return call(
        body,
        [jax.ShapeDtypeStruct(pieces.shape, BF16)],
        pieces.size * 4,
        pieces,
        scratch=(pltpu.VMEM(pieces.shape, F32),),
    )[0]


def back(own, reach, bcc, pieces, weight, norm_gain, place):
    tokens, width = own.shape
    columns = weight.shape[0]
    return pl.pallas_call(
        back_kernel,
        out_shape=jax.ShapeDtypeStruct((columns + 8 * 16, tokens), BF16),
        in_specs=[pl.BlockSpec(memory_space=pltpu.VMEM)] * 6
        + [pl.BlockSpec(memory_space=pltpu.SMEM)],
        out_specs=pl.BlockSpec(memory_space=pltpu.VMEM),
        scratch_shapes=[
            pltpu.VMEM(pieces.shape, F32),
            pltpu.VMEM((STATE, width), F32),
            pltpu.VMEM((tokens, width), BF16),
        ],
        compiler_params=pltpu.CompilerParams(vmem_limit_bytes=40 * 2**20),
        cost_estimate=pl.CostEstimate(
            flops=2 * tokens * width * (columns + STATE), bytes_accessed=10**7, transcendentals=0
        ),
        interpret=INTERPRET,
    )(own, reach, bcc, pieces, weight, norm_gain[None], place)


def scaled(summed):
    rows, tokens = summed.shape
    return call(
        scale_kernel, [jax.ShapeDtypeStruct((tokens, rows - 16), BF16)], rows * tokens, summed
    )[0]


def on_device(
    x_in, bc_in, z_gate, dt_in, conv_x, conv_bc, dt_bias, a_log, d_skip, norm_gain, out_weight
):
    tokens, width = x_in.shape
    count = lax.axis_size("seq")
    rim = jnp.concatenate([x_in[tokens - RIM :], bc_in[tokens - RIM :]], axis=1)
    rim = lax.ppermute(rim, "seq", [(i, i + 1) for i in range(count - 1)])
    weight = lax.all_gather(out_weight.T, "seq", axis=0, tiled=True)
    xc, bcc, cum, logstep, pieces = front(
        x_in, bc_in, rim, dt_in, conv_x, conv_bc, dt_bias, a_log
    )
    pieces = lax.all_to_all(pieces, "seq", 0, 0, tiled=True)
    own, reach = local(xc, bcc, cum, logstep, z_gate, d_skip)
    pieces = lax.all_to_all(scan(pieces, width), "seq", 0, 0, tiled=True)
    place = lax.axis_index("tp").astype(jnp.int32).reshape(1, 1)
    partial = back(own, reach, bcc, pieces, weight, norm_gain, place)
    return scaled(lax.psum_scatter(partial, "tp", scatter_dimension=0, tiled=True))


def solution(mesh):
    in_specs = (
        P("seq", "tp"),
        P("seq", None),
        P("seq", "tp"),
        P("seq", "tp"),
        P(None, "tp"),
        P(),
        P("tp"),
        P("tp"),
        P("tp"),
        P("tp"),
        P("tp", "seq"),
    )
    return jax.shard_map(
        on_device, mesh=mesh, in_specs=in_specs, out_specs=P("seq", "tp"), check_vma=False
    )
```

```python
import jax
import jax.numpy as jnp
from jax import lax
from jax.experimental import pallas as pl
from jax.experimental.pallas import tpu as pltpu
from jax.sharding import PartitionSpec as P

CHANNELS = 5120
HEADDIM = 64
STATE = 128
CONV = 4
CHUNK = 128
LANES = 128
RIM = 16
PAD_HEADS = 16
Z_RING = 16
PIECE = 48
EPSILON = 1e-05
HIGH = lax.Precision.HIGHEST
F32 = jnp.float32
BF16 = jnp.bfloat16
MASKED = -1e30
INTERPRET = False

NT = (((1,), (1,)), ((), ()))
TN = (((0,), (0,)), ((), ()))
NN = (((1,), (0,)), ((), ()))


def dot(a, b, dims=NN, precision=None):
    return lax.dot_general(a, b, dims, precision=precision, preferred_element_type=F32)


def call(body, outs, flops, *args, scratch=(), spaces=None):
    spaces = spaces or [pltpu.VMEM] * len(args)
    moved = sum(a.size * a.dtype.itemsize for a in args) + sum(
        o.size * o.dtype.itemsize for o in outs
    )
    return pl.pallas_call(
        body,
        out_shape=outs,
        in_specs=[pl.BlockSpec(memory_space=space) for space in spaces],
        out_specs=[pl.BlockSpec(memory_space=pltpu.VMEM)] * len(outs),
        scratch_shapes=list(scratch),
        compiler_params=pltpu.CompilerParams(vmem_limit_bytes=40 * 2**20),
        cost_estimate=pl.CostEstimate(flops=flops, bytes_accessed=moved, transcendentals=0),
        interpret=INTERPRET,
    )(*args)


def silu(v):
    half = 0.5 * v
    return half + half * jnp.tanh(half)


def split(v):
    hi = v.astype(BF16)
    return hi, (v - hi.astype(F32)).astype(BF16)


def iota(shape, dim):
    return lax.broadcasted_iota(jnp.int32, shape, dim)


def as_column(row):
    heads = row.shape[1]
    same = iota((PAD_HEADS, heads), 0) == iota((PAD_HEADS, heads), 1)
    return jnp.sum(jnp.where(same, row, 0.0), axis=1, keepdims=True)


def head_spread(width, dtype):
    return (iota((PAD_HEADS, width), 1) // HEADDIM == iota((PAD_HEADS, width), 0)).astype(dtype)


def spread_tokens(per_head, spread2):
    hi, lo = split(per_head)
    return dot(jnp.concatenate([hi, lo], axis=0), spread2, TN)


def spread_row(column, spread_f32):
    return jnp.sum(spread_f32 * column, axis=0, keepdims=True)


def fetch(sems, *pairs):
    copies = [pltpu.make_async_copy(a, b, sems.at[i]) for i, (a, b) in enumerate(pairs)]
    for copy in copies:
        copy.start()
    return copies


def conv_silu(padded, taps_ref, at, rows):
    first = 8 - (CONV - 1) + at
    total = taps_ref[0:1, :] * padded[first : first + rows, :]
    for k in range(1, CONV):
        total += taps_ref[k : k + 1, :] * padded[first + k : first + k + rows, :]
    return silu(total).astype(BF16)


def front_kernel(
    x_hbm, bc_hbm, dt_hbm, tap_x_hbm, tap_bc_hbm, bias_hbm, alog_hbm,
    xc_ref, bcc_ref, cum_ref, logstep_ref, state_ref, tail_ref,
    x_ref, bc_ref, dt_ref, tap_x_ref, tap_bc_ref, bias_ref, alog_ref,
    x_scr, bc_scr, logit_scr, fed_scr, sems,
):
    copies = fetch(
        sems, (dt_hbm, dt_ref), (bias_hbm, bias_ref), (alog_hbm, alog_ref), (bc_hbm, bc_ref),
        (tap_bc_hbm, tap_bc_ref), (tap_x_hbm, tap_x_ref), (x_hbm, x_ref),
    )
    tokens, width = x_ref.shape
    heads = dt_ref.shape[0]
    for copy in copies[:3]:
        copy.wait()
    logit_scr[...] = jnp.zeros_like(logit_scr)
    logit_scr[0:heads, :] = dt_ref[...].astype(F32)
    logits = logit_scr[...] + as_column(bias_ref[...])
    small = jnp.exp(-jnp.abs(logits))
    series = small * (1.0 - small * (0.5 - small * (1.0 / 3.0 - small * 0.25)))
    step = jnp.maximum(logits, 0.0) + jnp.where(small < 0.015625, series, jnp.log(1.0 + small))
    logstep = jnp.log(step)
    rate = -jnp.exp(as_column(alog_ref[...])) * step
    upto = (iota((CHUNK, CHUNK), 0) <= iota((CHUNK, CHUNK), 1)).astype(F32)
    run = jnp.zeros((PAD_HEADS, 1), F32)
    sums = []
    for at in range(0, tokens, CHUNK):
        within = dot(rate[:, at : at + CHUNK], upto, precision=HIGH) + run
        run = within[:, CHUNK - 1 :]
        sums.append(within)
    cum = jnp.concatenate(sums, axis=1)
    cum_ref[...] = cum
    logstep_ref[...] = logstep
    spread = head_spread(width, BF16)
    tail = spread_tokens(jnp.exp(run - cum + logstep), jnp.concatenate([spread, spread], axis=0))
    tail_ref[...] = tail[:RIM, :]

    for copy in copies[3:]:
        copy.wait()
    bc_scr[0:8, :] = jnp.zeros((8, bc_scr.shape[1]), F32)
    bc_scr[8:, :] = bc_ref[...].astype(F32)
    x_scr[0:8, :] = jnp.zeros((8, width), F32)
    x_scr[8:, :] = x_ref[...].astype(F32)
    for at in range(0, tokens, CHUNK):
        rows = slice(at, at + CHUNK)
        bcc_ref[rows, :] = conv_silu(bc_scr, tap_bc_ref, at, CHUNK)
        xc = conv_silu(x_scr, tap_x_ref, at, CHUNK)
        xc_ref[rows, :] = xc
        fed_scr[rows, :] = (xc.astype(F32) * tail[rows, :]).astype(BF16)
    fed_scr[0:RIM, :] = jnp.zeros((RIM, width), BF16)
    state_ref[...] = dot(bcc_ref[:, :STATE], fed_scr[...], TN)


def pack_decay(total, width):
    spread = head_spread(width, F32)
    hi, lo = split(total)
    even = iota((1, width), 1) % 2 == 0
    return jnp.where(even, spread_row(hi.astype(F32), spread), spread_row(lo.astype(F32), spread))


def rim_kernel(
    rim_ref, x_hbm, bc_hbm, tap_x_hbm, tap_bc_hbm, cum_ref, tail_ref, state_ref,
    xc_ref, bcc_ref, piece_ref, x_ref, bc_ref, tap_x_ref, tap_bc_ref, x_scr, bc_scr, piece_scr, sems,
):
    copies = fetch(
        sems, (x_hbm.at[0:RIM, :], x_ref), (bc_hbm.at[0:RIM, :], bc_ref),
        (tap_x_hbm, tap_x_ref), (tap_bc_hbm, tap_bc_ref),
    )
    width = x_ref.shape[1]
    rim = rim_ref[...].astype(F32)
    x_scr[0:8, :] = rim[RIM - 8 :, :width]
    bc_scr[0:8, :] = rim[RIM - 8 :, width:]
    last = cum_ref.shape[1] - 1
    decay = pack_decay(cum_ref[:, last:], width)
    for copy in copies:
        copy.wait()
    x_scr[8:, :] = x_ref[...].astype(F32)
    bc_scr[8:, :] = bc_ref[...].astype(F32)
    xc = conv_silu(x_scr, tap_x_ref, 0, RIM)
    bcc = conv_silu(bc_scr, tap_bc_ref, 0, RIM)
    xc_ref[...] = xc
    bcc_ref[...] = bcc
    fed = (xc.astype(F32) * tail_ref[...]).astype(BF16)
    state = state_ref[...] + dot(bcc[:, :STATE], fed, TN)
    each = STATE // Z_RING
    blocks = width // LANES
    for j in range(Z_RING):
        for b in range(blocks):
            at = j * PIECE + b * each
            piece_scr[at : at + each, :] = state[
                j * each : (j + 1) * each, b * LANES : (b + 1) * LANES
            ]
        at = j * PIECE + blocks * each
        piece_scr[at : at + 8, :] = jnp.zeros((8, LANES), F32)
        for b in range(blocks):
            piece_scr[at + b : at + b + 1, :] = decay[:, b * LANES : (b + 1) * LANES]
    piece_ref[...] = piece_scr[...].astype(BF16)


def local_kernel(
    xc_ref, xc_rim_ref, bcc_ref, bcc_rim_ref, cum_ref, logstep_ref, z_hbm, skip_hbm,
    own_ref, reach_ref, c_ref, held, xs, bs, z_ref, skip_ref, sems,
):
    copies = fetch(sems, (skip_hbm, skip_ref), (z_hbm, z_ref))
    tokens, width = xc_ref.shape
    xs[...] = xc_ref[...]
    xs[0:RIM, :] = xc_rim_ref[...]
    bs[...] = bcc_ref[...]
    bs[0:RIM, :] = bcc_rim_ref[...]
    c_ref[...] = bs[:, STATE:]
    spread = head_spread(width, BF16)
    spread2 = jnp.concatenate([spread, spread], axis=0)
    spread_f = head_spread(width, F32)
    causal = iota((CHUNK, CHUNK), 0) >= iota((CHUNK, CHUNK), 1)
    left = iota((CHUNK, LANES), 1) < HEADDIM
    held[...] = jnp.zeros_like(held)
    before = jnp.zeros((PAD_HEADS, 1), F32)
    for copy in copies:
        copy.wait()
    skip = spread_row(as_column(skip_ref[...]), spread_f)
    for at in range(0, tokens, CHUNK):
        rows = slice(at, at + CHUNK)
        b_part, c_part = bs[rows, :STATE], bs[rows, STATE:]
        cum = cum_ref[:, rows]
        source = logstep_ref[:, rows] - cum
        cum_cols = cum.T
        last = cum[:, CHUNK - 1 :]
        cb = dot(c_part, b_part, NT)
        gate = silu(z_ref[rows, :].astype(F32))
        reach_ref[rows, :] = spread_tokens(jnp.exp(cum), spread2) * gate
        fresh = spread_tokens(jnp.exp(cum - before), spread2)
        carried = dot(c_part, held[...].astype(BF16)) * fresh
        for pair in range(width // LANES):
            cols = slice(pair * LANES, (pair + 1) * LANES)
            mixes = []
            for head in (2 * pair, 2 * pair + 1):
                power = cum_cols[:, head : head + 1] + source[head : head + 1, :]
                mixes.append((cb * jnp.exp(jnp.where(causal, power, MASKED))).astype(BF16))
            x_part = xs[rows, cols]
            blank = jnp.zeros_like(x_part)
            x_two = jnp.concatenate(
                [jnp.where(left, x_part, blank), jnp.where(left, blank, x_part)], axis=0
            )
            y = dot(jnp.concatenate(mixes, axis=1), x_two) + carried[:, cols]
            y += skip[:, cols] * x_part.astype(F32)
            own_ref[rows, cols] = y * gate[:, cols]
        if at + CHUNK < tokens:
            tail = spread_tokens(jnp.exp(last + source), spread2)
            fed = (xs[rows, :].astype(F32) * tail).astype(BF16)
            kept = spread_row(jnp.exp(last - before), spread_f)
            held[...] = held[...] * kept + dot(b_part, fed, TN)
            before = last


def decay_rows(wide, at):
    both = wide[at : at + 8, :]
    even = iota((8, LANES), 1) % 2 == 0
    return both + jnp.where(even, pltpu.roll(both, LANES - 1, 1), pltpu.roll(both, 1, 1))


def total_kernel(blocks, in_ref, out_ref, wide):
    wide[...] = in_ref[...].astype(F32)
    carry = [jnp.zeros((8, LANES), F32)] * blocks
    passed = jnp.zeros((8, LANES), F32)
    for place in range(Z_RING):
        at = place * PIECE
        logs = decay_rows(wide, at + 8 * blocks)
        passed += logs
        kept = jnp.exp(logs)
        carry = [
            kept[b : b + 1, :] * carry[b] + wide[at + 8 * b : at + 8 * b + 8, :]
            for b in range(blocks)
        ]
    for peer in range(out_ref.shape[0]):
        for b in range(blocks):
            out_ref[peer, 8 * b : 8 * b + 8, :] = carry[b]
        out_ref[peer, 8 * blocks : 8 * blocks + 8, :] = passed


def scan_kernel(blocks, in_ref, total_ref, place_ref, out_ref, wide):
    wide[...] = in_ref[...].astype(F32)
    carry = [jnp.zeros((8, LANES), F32)] * blocks
    for peer in range(total_ref.shape[0] - 1):
        earlier = peer < place_ref[0, 0]
        kept = jnp.exp(total_ref[peer, 8 * blocks : 8 * blocks + 8, :])
        carry = [
            jnp.where(
                earlier,
                kept[b : b + 1, :] * carry[b] + total_ref[peer, 8 * b : 8 * b + 8, :],
                carry[b],
            )
            for b in range(blocks)
        ]
    for place in range(Z_RING):
        at = place * PIECE
        kept = jnp.exp(decay_rows(wide, at + 8 * blocks))
        for b in range(blocks):
            part = wide[at + 8 * b : at + 8 * b + 8, :]
            wide[at + 8 * b : at + 8 * b + 8, :] = carry[b]
            carry[b] = kept[b : b + 1, :] * carry[b] + part
    out_ref[...] = wide[...].astype(BF16)


def back_kernel(
    own_ref, reach_ref, c_ref, piece_ref, w_hbm, gain_ref, place_ref, out_hbm,
    wide, state, gated, w_ref, acc, stage, sems, out_sems,
):
    columns = w_ref.shape[0]
    span = columns // 2
    copies = fetch(
        sems,
        *[(w_hbm.at[k * span : (k + 1) * span, :], w_ref.at[k * span : (k + 1) * span, :])
          for k in range(2)],
    )
    tokens, width = own_ref.shape
    blocks = width // LANES
    each = STATE // Z_RING
    wide[...] = piece_ref[...].astype(F32)
    for j in range(Z_RING):
        for b in range(blocks):
            at = j * PIECE + b * each
            state[j * each : (j + 1) * each, b * LANES : (b + 1) * LANES] = wide[at : at + each, :]
    incoming = state[...].astype(BF16)
    ones = jnp.ones((16, 2 * width), BF16)
    totals = []
    for at in range(0, tokens, CHUNK):
        rows = slice(at, at + CHUNK)
        y = own_ref[rows, :] + reach_ref[rows, :] * dot(c_ref[rows, :], incoming)
        gated[rows, :] = (y * gain_ref[...]).astype(BF16)
        hi, lo = split(y * y)
        totals.append(dot(ones, jnp.concatenate([hi, lo], axis=1), NT))
    hi, lo = split(jnp.concatenate(totals, axis=1))
    row = iota((16, tokens), 0)
    mine = 2 * place_ref[0, 1]
    zero = jnp.zeros((16, tokens), F32)
    squares = jnp.where(
        row == mine, hi.astype(F32), jnp.where(row == mine + 1, lo.astype(F32), zero)
    ).astype(BF16)
    targets = 8
    block = columns // targets
    shard = columns // 64
    per_z = columns // Z_RING
    sent = []
    for half in range(2):
        copies[half].wait()
        acc[...] = dot(w_ref[half * span : (half + 1) * span, :], gated[...], NT)
        for x in range(targets // 2):
            d = 2 * x + half
            to = d * (block + 16)
            stage[to : to + block, :] = jnp.concatenate(
                [
                    acc[z * per_z + x * shard : z * per_z + (x + 1) * shard, :]
                    for z in range(Z_RING // 2)
                ],
                axis=0,
            ).astype(BF16)
            stage[to + block : to + block + 16, :] = squares
            part = pl.ds(to, block + 16)
            copy = pltpu.make_async_copy(stage.at[part, :], out_hbm.at[part, :], out_sems.at[d])
            copy.start()
            sent.append(copy)
    for copy in sent:
        copy.wait()


def scale_kernel(in_ref, out_ref):
    each = out_ref.shape[0]
    total = jnp.sum(in_ref[each:, :].astype(F32), axis=0, keepdims=True)
    scale = lax.rsqrt(total / CHANNELS + EPSILON)
    out_ref[...] = (in_ref[:each, :].astype(F32) * scale).astype(BF16)


def shaped(shape, dtype):
    return jax.ShapeDtypeStruct(shape, dtype)


def held_like(*arrays):
    return tuple(pltpu.VMEM(a.shape, a.dtype) for a in arrays)


def front(x_in, bc_in, dt_t, conv_x, conv_bc, dt_bias, a_log):
    tokens, width = x_in.shape
    args = (x_in, bc_in, dt_t, conv_x, conv_bc, dt_bias, a_log)
    return call(
        front_kernel,
        [
            shaped((tokens, width), BF16),
            shaped((tokens, 2 * STATE), BF16),
            shaped((PAD_HEADS, tokens), F32),
            shaped((PAD_HEADS, tokens), F32),
            shaped((STATE, width), F32),
            shaped((RIM, width), F32),
        ],
        8 * tokens * width * STATE,
        *args,
        spaces=[pl.ANY] * 7,
        scratch=held_like(*args)
        + (
            pltpu.VMEM((tokens + 8, width), F32),
            pltpu.VMEM((tokens + 8, 2 * STATE), F32),
            pltpu.VMEM((PAD_HEADS, tokens), F32),
            pltpu.VMEM((tokens, width), BF16),
            pltpu.SemaphoreType.DMA((7,)),
        ),
    )


def add_rim(rim, x_in, bc_in, conv_x, conv_bc, cum, tail, state):
    width = x_in.shape[1]
    return call(
        rim_kernel,
        [
            shaped((RIM, width), BF16),
            shaped((RIM, 2 * STATE), BF16),
            shaped((Z_RING * PIECE, LANES), BF16),
        ],
        2 * 128 * width * STATE,
        rim, x_in, bc_in, conv_x, conv_bc, cum, tail, state,
        spaces=[pltpu.VMEM] + [pl.ANY] * 4 + [pltpu.VMEM] * 3,
        scratch=(
            pltpu.VMEM((RIM, width), BF16),
            pltpu.VMEM((RIM, 2 * STATE), BF16),
            *held_like(conv_x, conv_bc),
            pltpu.VMEM((RIM + 8, width), F32),
            pltpu.VMEM((RIM + 8, 2 * STATE), F32),
            pltpu.VMEM((Z_RING * PIECE, LANES), F32),
            pltpu.SemaphoreType.DMA((4,)),
        ),
    )


def local(xc, xc_rim, bcc, bcc_rim, cum, logstep, z_gate, d_skip):
    tokens, width = xc.shape
    return call(
        local_kernel,
        [shaped((tokens, width), F32)] * 2 + [shaped((tokens, STATE), BF16)],
        12 * tokens * width * STATE,
        xc, xc_rim, bcc, bcc_rim, cum, logstep, z_gate, d_skip,
        spaces=[pltpu.VMEM] * 6 + [pl.ANY] * 2,
        scratch=(pltpu.VMEM((STATE, width), F32),)
        + held_like(xc, bcc, z_gate, d_skip)
        + (pltpu.SemaphoreType.DMA((2,)),),
    )


def row_total(pieces, width, peers):
    def body(*refs):
        total_kernel(width // LANES, *refs)

    return call(
        body,
        [shaped((peers, PIECE, LANES), F32)],
        pieces.size * 4,
        pieces,
        scratch=(pltpu.VMEM(pieces.shape, F32),),
    )[0]


def scan(pieces, totals, place, width):
    def body(*refs):
        scan_kernel(width // LANES, *refs)

    return call(
        body,
        [shaped(pieces.shape, BF16)],
        pieces.size * 4,
        pieces, totals, place,
        spaces=[pltpu.VMEM, pltpu.VMEM, pltpu.SMEM],
        scratch=(pltpu.VMEM(pieces.shape, F32),),
    )[0]


def back(own, reach, c_part, pieces, weight, norm_gain, place):
    tokens, width = own.shape
    columns = weight.shape[0]
    out = shaped((columns + 8 * 16, tokens), BF16)
    return pl.pallas_call(
        back_kernel,
        out_shape=out,
        in_specs=[pl.BlockSpec(memory_space=pltpu.VMEM)] * 4
        + [
            pl.BlockSpec(memory_space=pl.ANY),
            pl.BlockSpec(memory_space=pltpu.VMEM),
            pl.BlockSpec(memory_space=pltpu.SMEM),
        ],
        out_specs=pl.BlockSpec(memory_space=pl.ANY),
        scratch_shapes=[
            pltpu.VMEM(pieces.shape, F32),
            pltpu.VMEM((STATE, width), F32),
            pltpu.VMEM((tokens, width), BF16),
            *held_like(weight),
            pltpu.VMEM((columns // 2, tokens), F32),
            *held_like(out),
            pltpu.SemaphoreType.DMA((2,)),
            pltpu.SemaphoreType.DMA((8,)),
        ],
        compiler_params=pltpu.CompilerParams(vmem_limit_bytes=40 * 2**20),
        cost_estimate=pl.CostEstimate(
            flops=2 * tokens * width * (columns + STATE), bytes_accessed=10**7, transcendentals=0
        ),
        interpret=INTERPRET,
    )(own, reach, c_part, pieces, weight, norm_gain[None], place)


def scaled(summed):
    rows, tokens = summed.shape
    return call(scale_kernel, [shaped((rows - 16, tokens), BF16)], rows * tokens, summed)[0]


def on_device(
    x_in, bc_in, z_gate, dt_in, conv_x, conv_bc, dt_bias, a_log, d_skip, norm_gain, out_weight
):
    tokens, width = x_in.shape
    count = lax.axis_size("seq")
    rows = count // Z_RING
    along_z = [[x * Z_RING + z for z in range(Z_RING)] for x in range(rows)]
    along_x = [[x * Z_RING + z for x in range(rows)] for z in range(Z_RING)]
    weight = lax.all_gather(
        out_weight.T, "seq", axis=0, tiled=True, axis_index_groups=along_x
    )
    weight = lax.all_gather(weight, "seq", axis=0, tiled=True, axis_index_groups=along_z)
    rim = jnp.concatenate([x_in[tokens - RIM :], bc_in[tokens - RIM :]], axis=1)
    rim = lax.ppermute(rim, "seq", [(i, i + 1) for i in range(count - 1)])
    place = jnp.stack(
        [lax.axis_index("seq") // Z_RING, lax.axis_index("tp")]
    ).astype(jnp.int32)[None]

    xc, bcc, cum, logstep, state, tail = front(
        x_in, bc_in, dt_in.T, conv_x, conv_bc, dt_bias[None], a_log[None]
    )
    xc_rim, bcc_rim, pieces = add_rim(rim, x_in, bc_in, conv_x, conv_bc, cum, tail, state)
    pieces = lax.all_to_all(pieces, "seq", 0, 0, tiled=True, axis_index_groups=along_z)
    totals = row_total(pieces, width, rows)
    totals = lax.all_to_all(totals, "seq", 0, 0, tiled=True, axis_index_groups=along_x)
    pieces = scan(pieces, totals, place, width)
    pieces = lax.all_to_all(pieces, "seq", 0, 0, tiled=True, axis_index_groups=along_z)
    own, reach, c_part = local(xc, xc_rim, bcc, bcc_rim, cum, logstep, z_gate, d_skip[None])
    partial = back(own, reach, c_part, pieces, weight, norm_gain, place)
    return scaled(lax.psum_scatter(partial, "tp", scatter_dimension=0, tiled=True)).T


def solution(mesh):
    in_specs = (
        P("seq", "tp"),
        P("seq", None),
        P("seq", "tp"),
        P("seq", "tp"),
        P(None, "tp"),
        P(),
        P("tp"),
        P("tp"),
        P("tp"),
        P("tp"),
        P("tp", "seq"),
    )
    return jax.shard_map(
        on_device, mesh=mesh, in_specs=in_specs, out_specs=P("seq", "tp"), check_vma=False
    )
```

```python
import jax
import jax.numpy as jnp
from jax import lax
from jax.experimental import pallas as pl
from jax.experimental.pallas import tpu as pltpu
from jax.sharding import PartitionSpec as P

CHANNELS = 5120
HEADDIM = 64
STATE = 128
CONV = 4
CHUNK = 128
LANES = 128
RIM = 16
PAD_HEADS = 16
Z_RING = 16
PIECE = 48
TARGETS = 8
FULL = 63
EPSILON = 1e-05
HIGH = lax.Precision.HIGHEST
F32 = jnp.float32
BF16 = jnp.bfloat16
MASKED = -1e30
INTERPRET = False

NT = (((1,), (1,)), ((), ()))
TN = (((0,), (0,)), ((), ()))
NN = (((1,), (0,)), ((), ()))


def dot(a, b, dims=NN, precision=None):
    return lax.dot_general(a, b, dims, precision=precision, preferred_element_type=F32)


def call(
    body, outs, flops, *args, scratch=(), spaces=None, out_spaces=None, aliases=None, vmem=40
):
    spaces = spaces or [pltpu.VMEM] * len(args)
    out_spaces = out_spaces or [pltpu.VMEM] * len(outs)
    moved = sum(a.size * a.dtype.itemsize for a in args) + sum(
        o.size * o.dtype.itemsize for o in outs
    )
    return pl.pallas_call(
        body,
        out_shape=outs,
        in_specs=[pl.BlockSpec(memory_space=space) for space in spaces],
        out_specs=[pl.BlockSpec(memory_space=space) for space in out_spaces],
        input_output_aliases=aliases or {},
        scratch_shapes=list(scratch),
        compiler_params=pltpu.CompilerParams(vmem_limit_bytes=vmem * 2**20),
        cost_estimate=pl.CostEstimate(flops=flops, bytes_accessed=moved, transcendentals=0),
        interpret=INTERPRET,
    )(*args)


def silu(v):
    half = 0.5 * v
    return half + half * jnp.tanh(half)


def split(v):
    hi = v.astype(BF16)
    return hi, (v - hi.astype(F32)).astype(BF16)


def iota(shape, dim):
    return lax.broadcasted_iota(jnp.int32, shape, dim)


def as_column(row):
    heads = row.shape[1]
    same = iota((PAD_HEADS, heads), 0) == iota((PAD_HEADS, heads), 1)
    return jnp.sum(jnp.where(same, row, 0.0), axis=1, keepdims=True)


def head_spread(width, dtype):
    return (iota((PAD_HEADS, width), 1) // HEADDIM == iota((PAD_HEADS, width), 0)).astype(dtype)


def spread_tokens(per_head, spread2):
    hi, lo = split(per_head)
    return dot(jnp.concatenate([hi, lo], axis=0), spread2, TN)


def spread_row(column, spread_f32):
    return jnp.sum(spread_f32 * column, axis=0, keepdims=True)


def fetch(sems, *pairs):
    copies = [pltpu.make_async_copy(a, b, sems.at[i]) for i, (a, b) in enumerate(pairs)]
    for copy in copies:
        copy.start()
    return copies


def conv_silu(padded, taps_ref, at, rows):
    first = 8 - (CONV - 1) + at
    total = taps_ref[0:1, :] * padded[first : first + rows, :]
    for k in range(1, CONV):
        total += taps_ref[k : k + 1, :] * padded[first + k : first + k + rows, :]
    return silu(total).astype(BF16)


def front_kernel(
    x_hbm, bc_hbm, dt_hbm, tap_x_hbm, tap_bc_hbm, bias_hbm, alog_hbm,
    xc_ref, bcc_ref, cum_ref, logstep_ref, state_ref, tail_ref,
    x_ref, bc_ref, dt_ref, tap_x_ref, tap_bc_ref, bias_ref, alog_ref,
    x_scr, bc_scr, logit_scr, fed_scr, sems,
):
    copies = fetch(
        sems, (dt_hbm, dt_ref), (bias_hbm, bias_ref), (alog_hbm, alog_ref), (bc_hbm, bc_ref),
        (tap_bc_hbm, tap_bc_ref), (tap_x_hbm, tap_x_ref), (x_hbm, x_ref),
    )
    tokens, width = x_ref.shape
    heads = dt_ref.shape[0]
    for copy in copies[:3]:
        copy.wait()
    logit_scr[...] = jnp.zeros_like(logit_scr)
    logit_scr[0:heads, :] = dt_ref[...].astype(F32)
    logits = logit_scr[...] + as_column(bias_ref[...])
    small = jnp.exp(-jnp.abs(logits))
    series = small * (1.0 - small * (0.5 - small * (1.0 / 3.0 - small * 0.25)))
    step = jnp.maximum(logits, 0.0) + jnp.where(small < 0.015625, series, jnp.log(1.0 + small))
    logstep = jnp.log(step)
    rate = -jnp.exp(as_column(alog_ref[...])) * step
    upto = (iota((CHUNK, CHUNK), 0) <= iota((CHUNK, CHUNK), 1)).astype(F32)
    run = jnp.zeros((PAD_HEADS, 1), F32)
    sums = []
    for at in range(0, tokens, CHUNK):
        within = dot(rate[:, at : at + CHUNK], upto, precision=HIGH) + run
        run = within[:, CHUNK - 1 :]
        sums.append(within)
    cum = jnp.concatenate(sums, axis=1)
    cum_ref[...] = cum
    logstep_ref[...] = logstep
    spread = head_spread(width, BF16)
    tail = spread_tokens(jnp.exp(run - cum + logstep), jnp.concatenate([spread, spread], axis=0))
    tail_ref[...] = tail[:RIM, :]

    for copy in copies[3:]:
        copy.wait()
    bc_scr[0:8, :] = jnp.zeros((8, bc_scr.shape[1]), F32)
    bc_scr[8:, :] = bc_ref[...].astype(F32)
    x_scr[0:8, :] = jnp.zeros((8, width), F32)
    x_scr[8:, :] = x_ref[...].astype(F32)
    for at in range(0, tokens, CHUNK):
        rows = slice(at, at + CHUNK)
        bcc_ref[rows, :] = conv_silu(bc_scr, tap_bc_ref, at, CHUNK)
        xc = conv_silu(x_scr, tap_x_ref, at, CHUNK)
        xc_ref[rows, :] = xc
        fed_scr[rows, :] = (xc.astype(F32) * tail[rows, :]).astype(BF16)
    fed_scr[0:RIM, :] = jnp.zeros((RIM, width), BF16)
    state_ref[...] = dot(bcc_ref[:, :STATE], fed_scr[...], TN)


def pack_decay(total, width):
    spread = head_spread(width, F32)
    hi, lo = split(total)
    even = iota((1, width), 1) % 2 == 0
    return jnp.where(even, spread_row(hi.astype(F32), spread), spread_row(lo.astype(F32), spread))


def rim_kernel(
    rim_ref, x_hbm, bc_hbm, tap_x_hbm, tap_bc_hbm, cum_ref, tail_ref, state_ref,
    xc_ref, bcc_ref, piece_ref, x_ref, bc_ref, tap_x_ref, tap_bc_ref, x_scr, bc_scr, piece_scr, sems,
):
    copies = fetch(
        sems, (x_hbm.at[0:RIM, :], x_ref), (bc_hbm.at[0:RIM, :], bc_ref),
        (tap_x_hbm, tap_x_ref), (tap_bc_hbm, tap_bc_ref),
    )
    width = x_ref.shape[1]
    rim = rim_ref[...].astype(F32)
    x_scr[0:8, :] = rim[RIM - 8 :, :width]
    bc_scr[0:8, :] = rim[RIM - 8 :, width:]
    last = cum_ref.shape[1] - 1
    decay = pack_decay(cum_ref[:, last:], width)
    for copy in copies:
        copy.wait()
    x_scr[8:, :] = x_ref[...].astype(F32)
    bc_scr[8:, :] = bc_ref[...].astype(F32)
    xc = conv_silu(x_scr, tap_x_ref, 0, RIM)
    bcc = conv_silu(bc_scr, tap_bc_ref, 0, RIM)
    xc_ref[...] = xc
    bcc_ref[...] = bcc
    fed = (xc.astype(F32) * tail_ref[...]).astype(BF16)
    state = state_ref[...] + dot(bcc[:, :STATE], fed, TN)
    each = STATE // Z_RING
    blocks = width // LANES
    for j in range(Z_RING):
        for b in range(blocks):
            at = j * PIECE + b * each
            piece_scr[at : at + each, :] = state[
                j * each : (j + 1) * each, b * LANES : (b + 1) * LANES
            ]
        at = j * PIECE + blocks * each
        piece_scr[at : at + 8, :] = jnp.zeros((8, LANES), F32)
        for b in range(blocks):
            piece_scr[at + b : at + b + 1, :] = decay[:, b * LANES : (b + 1) * LANES]
    piece_ref[...] = piece_scr[...].astype(BF16)


def local_kernel(
    xc_ref, xc_rim_ref, bcc_ref, bcc_rim_ref, cum_ref, logstep_ref, z_hbm, skip_hbm, w_ref,
    own_ref, reach_ref, c_ref, w_out_ref, held, xs, bs, z_ref, skip_ref, sems,
):
    del w_ref, w_out_ref
    copies = fetch(sems, (skip_hbm, skip_ref), (z_hbm, z_ref))
    tokens, width = xc_ref.shape
    xs[...] = xc_ref[...]
    xs[0:RIM, :] = xc_rim_ref[...]
    bs[...] = bcc_ref[...]
    bs[0:RIM, :] = bcc_rim_ref[...]
    c_ref[...] = bs[:, STATE:]
    spread = head_spread(width, BF16)
    spread2 = jnp.concatenate([spread, spread], axis=0)
    spread_f = head_spread(width, F32)
    causal = iota((CHUNK, CHUNK), 0) >= iota((CHUNK, CHUNK), 1)
    left = iota((CHUNK, LANES), 1) < HEADDIM
    held[...] = jnp.zeros_like(held)
    before = jnp.zeros((PAD_HEADS, 1), F32)
    for copy in copies:
        copy.wait()
    skip = spread_row(as_column(skip_ref[...]), spread_f)
    for at in range(0, tokens, CHUNK):
        rows = slice(at, at + CHUNK)
        b_part, c_part = bs[rows, :STATE], bs[rows, STATE:]
        cum = cum_ref[:, rows]
        source = logstep_ref[:, rows] - cum
        cum_cols = cum.T
        last = cum[:, CHUNK - 1 :]
        cb = dot(c_part, b_part, NT)
        gate = silu(z_ref[rows, :].astype(F32))
        reach_ref[rows, :] = spread_tokens(jnp.exp(cum), spread2) * gate
        fresh = spread_tokens(jnp.exp(cum - before), spread2)
        carried = dot(c_part, held[...].astype(BF16)) * fresh
        for pair in range(width // LANES):
            cols = slice(pair * LANES, (pair + 1) * LANES)
            mixes = []
            for head in (2 * pair, 2 * pair + 1):
                power = cum_cols[:, head : head + 1] + source[head : head + 1, :]
                mixes.append((cb * jnp.exp(jnp.where(causal, power, MASKED))).astype(BF16))
            x_part = xs[rows, cols]
            blank = jnp.zeros_like(x_part)
            x_two = jnp.concatenate(
                [jnp.where(left, x_part, blank), jnp.where(left, blank, x_part)], axis=0
            )
            y = dot(jnp.concatenate(mixes, axis=1), x_two) + carried[:, cols]
            y += skip[:, cols] * x_part.astype(F32)
            own_ref[rows, cols] = y * gate[:, cols]
        if at + CHUNK < tokens:
            tail = spread_tokens(jnp.exp(last + source), spread2)
            fed = (xs[rows, :].astype(F32) * tail).astype(BF16)
            kept = spread_row(jnp.exp(last - before), spread_f)
            held[...] = held[...] * kept + dot(b_part, fed, TN)
            before = last


def decay_rows(wide, at):
    both = wide[at : at + 8, :]
    even = iota((8, LANES), 1) % 2 == 0
    return both + jnp.where(even, pltpu.roll(both, LANES - 1, 1), pltpu.roll(both, 1, 1))


def total_kernel(blocks, in_ref, after_ref, out_ref, wide):
    del after_ref
    wide[...] = in_ref[...].astype(F32)
    carry = [jnp.zeros((8, LANES), F32)] * blocks
    passed = jnp.zeros((8, LANES), F32)
    for place in range(Z_RING):
        at = place * PIECE
        logs = decay_rows(wide, at + 8 * blocks)
        passed += logs
        kept = jnp.exp(logs)
        carry = [
            kept[b : b + 1, :] * carry[b] + wide[at + 8 * b : at + 8 * b + 8, :]
            for b in range(blocks)
        ]
    for peer in range(out_ref.shape[0]):
        for b in range(blocks):
            out_ref[peer, 8 * b : 8 * b + 8, :] = carry[b]
        out_ref[peer, 8 * blocks : 8 * blocks + 8, :] = passed


def scan_kernel(blocks, in_ref, total_ref, place_ref, out_ref, wide):
    wide[...] = in_ref[...].astype(F32)
    carry = [jnp.zeros((8, LANES), F32)] * blocks
    for peer in range(total_ref.shape[0] - 1):
        earlier = peer < place_ref[0, 0]
        kept = jnp.exp(total_ref[peer, 8 * blocks : 8 * blocks + 8, :])
        carry = [
            jnp.where(
                earlier,
                kept[b : b + 1, :] * carry[b] + total_ref[peer, 8 * b : 8 * b + 8, :],
                carry[b],
            )
            for b in range(blocks)
        ]
    for place in range(Z_RING):
        at = place * PIECE
        kept = jnp.exp(decay_rows(wide, at + 8 * blocks))
        for b in range(blocks):
            part = wide[at + 8 * b : at + 8 * b + 8, :]
            wide[at + 8 * b : at + 8 * b + 8, :] = carry[b]
            carry[b] = kept[b : b + 1, :] * carry[b] + part
    out_ref[...] = wide[...].astype(BF16)


def rim_source_kernel(x_hbm, bc_hbm, out_ref, sems):
    tokens, width = x_hbm.shape
    for copy in fetch(
        sems,
        (x_hbm.at[tokens - RIM :, :], out_ref.at[:, 0:width]),
        (bc_hbm.at[tokens - RIM :, :], out_ref.at[:, width:]),
    ):
        copy.wait()


def fetch_half(w_hbm, w_ref, half, sems):
    block = w_hbm.shape[0] // TARGETS
    return fetch(
        sems,
        *[
            (
                w_hbm.at[pl.ds(pl.multiple_of((2 * y + half) * block, block), block), :],
                w_ref.at[y * block : (y + 1) * block, :],
            )
            for y in range(TARGETS // 2)
        ],
    )


def back_kernel(
    own_ref, reach_ref, c_ref, piece_ref, w_hbm, gain_ref, place_ref,
    out_ref, gated_ref, square_ref, wide, state, w_ref, sems,
):
    copies = fetch_half(w_hbm, w_ref, 1 - place_ref[0, 1] % 2, sems)
    tokens, width = own_ref.shape
    blocks = width // LANES
    each = STATE // Z_RING
    wide[...] = piece_ref[...].astype(F32)
    for j in range(Z_RING):
        for b in range(blocks):
            at = j * PIECE + b * each
            state[j * each : (j + 1) * each, b * LANES : (b + 1) * LANES] = wide[at : at + each, :]
    incoming = state[...].astype(BF16)
    ones = jnp.ones((16, 2 * width), BF16)
    totals = []
    for at in range(0, tokens, CHUNK):
        rows = slice(at, at + CHUNK)
        y = own_ref[rows, :] + reach_ref[rows, :] * dot(c_ref[rows, :], incoming)
        gated_ref[rows, :] = (y * gain_ref[...]).astype(BF16)
        hi, lo = split(y * y)
        totals.append(dot(ones, jnp.concatenate([hi, lo], axis=1), NT))
    hi, lo = split(jnp.concatenate(totals, axis=1))
    row = iota((16, tokens), 0)
    mine = 2 * place_ref[0, 1]
    zero = jnp.zeros((16, tokens), F32)
    squares = jnp.where(
        row == mine, hi.astype(F32), jnp.where(row == mine + 1, lo.astype(F32), zero)
    ).astype(BF16)
    square_ref[...] = squares
    for copy in copies:
        copy.wait()
    block = w_ref.shape[0] // (TARGETS // 2)
    for y in range(TARGETS // 2):
        to = y * (block + 16)
        out_ref[to : to + block, :] = dot(
            w_ref[y * block : (y + 1) * block, :], gated_ref[...], NT
        ).astype(BF16)
        out_ref[to + block : to + block + 16, :] = squares


def kept_kernel(gated_ref, w_hbm, place_ref, out_ref, w_ref, sems):
    copies = fetch_half(w_hbm, w_ref, place_ref[0, 1] % 2, sems)
    block = w_ref.shape[0] // (TARGETS // 2)
    for y in range(TARGETS // 2):
        rows = slice(y * block, (y + 1) * block)
        copies[y].wait()
        out_ref[rows, :] = dot(w_ref[rows, :], gated_ref[...], NT).astype(BF16)


def pair_kernel(kept_ref, got_ref, square_ref, out_ref):
    block = kept_ref.shape[0] // (TARGETS // 2)
    for y in range(TARGETS // 2):
        to = y * (block + 16)
        rows = slice(to, to + block)
        out_ref[rows, :] = (
            kept_ref[y * block : (y + 1) * block, :].astype(F32) + got_ref[rows, :].astype(F32)
        ).astype(BF16)
        rows = slice(to + block, to + block + 16)
        out_ref[rows, :] = (square_ref[...].astype(F32) + got_ref[rows, :].astype(F32)).astype(BF16)


def scale_kernel(in_ref, out_ref):
    block = out_ref.shape[0]
    parts = TARGETS // 2
    each = block + 16
    total = jnp.zeros((1, out_ref.shape[1]), F32)
    for y in range(parts):
        part = in_ref[y * each + block : (y + 1) * each, :].astype(F32)
        total += jnp.sum(part, axis=0, keepdims=True)
    scale = lax.rsqrt(total / CHANNELS + EPSILON)
    mixed = in_ref[0:block, :].astype(F32)
    for y in range(1, parts):
        mixed += in_ref[y * each : y * each + block, :].astype(F32)
    out_ref[...] = (mixed * scale).astype(BF16)


def shaped(shape, dtype):
    return jax.ShapeDtypeStruct(shape, dtype)


def held_like(*arrays):
    return tuple(pltpu.VMEM(a.shape, a.dtype) for a in arrays)


def front(x_in, bc_in, dt_t, conv_x, conv_bc, dt_bias, a_log):
    tokens, width = x_in.shape
    args = (x_in, bc_in, dt_t, conv_x, conv_bc, dt_bias, a_log)
    return call(
        front_kernel,
        [
            shaped((tokens, width), BF16),
            shaped((tokens, 2 * STATE), BF16),
            shaped((PAD_HEADS, tokens), F32),
            shaped((PAD_HEADS, tokens), F32),
            shaped((STATE, width), F32),
            shaped((RIM, width), F32),
        ],
        8 * tokens * width * STATE,
        *args,
        spaces=[pltpu.HBM] * 7,
        vmem=FULL,
        scratch=held_like(*args)
        + (
            pltpu.VMEM((tokens + 8, width), F32),
            pltpu.VMEM((tokens + 8, 2 * STATE), F32),
            pltpu.VMEM((PAD_HEADS, tokens), F32),
            pltpu.VMEM((tokens, width), BF16),
            pltpu.SemaphoreType.DMA((7,)),
        ),
    )


def add_rim(rim, x_in, bc_in, conv_x, conv_bc, cum, tail, state):
    width = x_in.shape[1]
    return call(
        rim_kernel,
        [
            shaped((RIM, width), BF16),
            shaped((RIM, 2 * STATE), BF16),
            shaped((Z_RING * PIECE, LANES), BF16),
        ],
        2 * 128 * width * STATE,
        rim, x_in, bc_in, conv_x, conv_bc, cum, tail, state,
        spaces=[pltpu.VMEM] + [pltpu.HBM] * 4 + [pltpu.VMEM] * 3,
        vmem=FULL,
        scratch=(
            pltpu.VMEM((RIM, width), BF16),
            pltpu.VMEM((RIM, 2 * STATE), BF16),
            *held_like(conv_x, conv_bc),
            pltpu.VMEM((RIM + 8, width), F32),
            pltpu.VMEM((RIM + 8, 2 * STATE), F32),
            pltpu.VMEM((Z_RING * PIECE, LANES), F32),
            pltpu.SemaphoreType.DMA((4,)),
        ),
    )


def local(xc, xc_rim, bcc, bcc_rim, cum, logstep, z_gate, d_skip, weight):
    tokens, width = xc.shape
    return call(
        local_kernel,
        [shaped((tokens, width), F32)] * 2
        + [shaped((tokens, STATE), BF16), shaped(weight.shape, BF16)],
        12 * tokens * width * STATE,
        xc, xc_rim, bcc, bcc_rim, cum, logstep, z_gate, d_skip, weight,
        spaces=[pltpu.VMEM] * 6 + [pltpu.HBM] * 3,
        out_spaces=[pltpu.VMEM] * 3 + [pltpu.HBM],
        aliases={8: 3},
        scratch=(pltpu.VMEM((STATE, width), F32),)
        + held_like(xc, bcc, z_gate, d_skip)
        + (pltpu.SemaphoreType.DMA((2,)),),
    )


def row_total(pieces, width, peers, after):
    def body(*refs):
        total_kernel(width // LANES, *refs)

    return call(
        body,
        [shaped((peers, PIECE, LANES), F32)],
        pieces.size * 4,
        pieces, after,
        spaces=[pltpu.VMEM, pl.ANY],
        scratch=(pltpu.VMEM(pieces.shape, F32),),
    )[0]


def scan(pieces, totals, place, width):
    def body(*refs):
        scan_kernel(width // LANES, *refs)

    return call(
        body,
        [shaped(pieces.shape, BF16)],
        pieces.size * 4,
        pieces, totals, place,
        spaces=[pltpu.VMEM, pltpu.VMEM, pltpu.SMEM],
        scratch=(pltpu.VMEM(pieces.shape, F32),),
    )[0]


def rim_source(x_in, bc_in):
    return call(
        rim_source_kernel,
        [shaped((RIM, x_in.shape[1] + bc_in.shape[1]), BF16)],
        0,
        x_in, bc_in,
        spaces=[pltpu.HBM] * 2,
        vmem=FULL,
        scratch=(pltpu.SemaphoreType.DMA((2,)),),
    )[0]


def back(own, reach, c_part, pieces, weight, norm_gain, place):
    tokens, width = own.shape
    columns = weight.shape[0]
    half = columns // 2
    parts = TARGETS // 2
    return call(
        back_kernel,
        [
            shaped((half + parts * 16, tokens), BF16),
            shaped((tokens, width), BF16),
            shaped((16, tokens), BF16),
        ],
        2 * tokens * width * (half + STATE),
        own, reach, c_part, pieces, weight, norm_gain[None], place,
        spaces=[pltpu.VMEM] * 4 + [pltpu.HBM, pltpu.VMEM, pltpu.SMEM],
        vmem=FULL - 5,
        scratch=(
            pltpu.VMEM(pieces.shape, F32),
            pltpu.VMEM((STATE, width), F32),
            pltpu.VMEM((half, width), BF16),
            pltpu.SemaphoreType.DMA((parts,)),
        ),
    )


def kept_part(gated, weight, place):
    tokens, width = gated.shape
    half = weight.shape[0] // 2
    return call(
        kept_kernel,
        [shaped((half, tokens), BF16)],
        2 * tokens * width * half,
        gated, weight, place,
        spaces=[pltpu.VMEM, pltpu.HBM, pltpu.SMEM],
        vmem=FULL - 2,
        scratch=(
            pltpu.VMEM((half, width), BF16),
            pltpu.SemaphoreType.DMA((TARGETS // 2,)),
        ),
    )[0]


def pair_sum(kept, got, squares):
    return call(pair_kernel, [shaped(got.shape, BF16)], got.size, kept, got, squares)[0]


def scaled(parts):
    rows, tokens = parts.shape
    block = rows // (TARGETS // 2) - 16
    return call(scale_kernel, [shaped((block, tokens), BF16)], rows * tokens, parts)[0]


def on_device(
    x_in, bc_in, z_gate, dt_in, conv_x, conv_bc, dt_bias, a_log, d_skip, norm_gain, out_weight
):
    tokens, width = x_in.shape
    count = lax.axis_size("seq")
    rows = count // Z_RING
    along_z = [[x * Z_RING + z for z in range(Z_RING)] for x in range(rows)]
    along_x = [[x * Z_RING + z for x in range(rows)] for z in range(Z_RING)]
    weight = lax.all_gather(
        out_weight.T, "seq", axis=0, tiled=True, axis_index_groups=along_z
    )
    rim = lax.ppermute(rim_source(x_in, bc_in), "seq", [(i, i + 1) for i in range(count - 1)])
    place = jnp.stack(
        [lax.axis_index("seq") // Z_RING, lax.axis_index("tp")]
    ).astype(jnp.int32)[None]

    xc, bcc, cum, logstep, state, tail = front(
        x_in, bc_in, dt_in.T, conv_x, conv_bc, dt_bias[None], a_log[None]
    )
    xc_rim, bcc_rim, pieces = add_rim(rim, x_in, bc_in, conv_x, conv_bc, cum, tail, state)
    pieces = lax.all_to_all(pieces, "seq", 0, 0, tiled=True, axis_index_groups=along_z)
    own, reach, c_part, weight = local(
        xc, xc_rim, bcc, bcc_rim, cum, logstep, z_gate, d_skip[None], weight
    )
    weight = lax.all_gather(weight, "seq", axis=0, tiled=True, axis_index_groups=along_x)
    totals = row_total(pieces, width, rows, c_part)
    totals = lax.all_to_all(totals, "seq", 0, 0, tiled=True, axis_index_groups=along_x)
    pieces = scan(pieces, totals, place, width)
    pieces = lax.all_to_all(pieces, "seq", 0, 0, tiled=True, axis_index_groups=along_z)

    given, gated, squares = back(own, reach, c_part, pieces, weight, norm_gain, place)
    got = lax.ppermute(given, "tp", [(i, i ^ 1) for i in range(TARGETS)])
    kept = kept_part(gated, weight, place)
    parts = pair_sum(kept, got, squares)
    along_y = [[core + 2 * y for y in range(TARGETS // 2)] for core in range(2)]
    parts = lax.all_to_all(parts, "tp", 0, 0, tiled=True, axis_index_groups=along_y)
    return scaled(parts).T


def solution(mesh):
    in_specs = (
        P("seq", "tp"),
        P("seq", None),
        P("seq", "tp"),
        P("seq", "tp"),
        P(None, "tp"),
        P(),
        P("tp"),
        P("tp"),
        P("tp"),
        P("tp"),
        P("tp", "seq"),
    )
    return jax.shard_map(
        on_device, mesh=mesh, in_specs=in_specs, out_specs=P("seq", "tp"), check_vma=False
    )
```

```python
import jax
import jax.numpy as jnp
from jax import lax
from jax.experimental import pallas as pl
from jax.experimental.pallas import tpu as pltpu
from jax.sharding import PartitionSpec as P

CHANNELS = 5120
HEADDIM = 64
STATE = 128
CONV = 4
CHUNK = 128
LANES = 128
RIM = 16
PAD_HEADS = 16
Z_RING = 16
PIECE = 48
TARGETS = 8
Z_STRIDE = 4
FULL = 63
EPSILON = 1e-05
HIGH = lax.Precision.HIGHEST
F32 = jnp.float32
BF16 = jnp.bfloat16
MASKED = -1e30
INTERPRET = False

NT = (((1,), (1,)), ((), ()))
TN = (((0,), (0,)), ((), ()))
NN = (((1,), (0,)), ((), ()))


def dot(a, b, dims=NN, precision=None):
    return lax.dot_general(a, b, dims, precision=precision, preferred_element_type=F32)


def call(
    body, outs, flops, *args, scratch=(), spaces=None, out_spaces=None, aliases=None, vmem=40
):
    spaces = spaces or [pltpu.VMEM] * len(args)
    out_spaces = out_spaces or [pltpu.VMEM] * len(outs)
    moved = sum(a.size * a.dtype.itemsize for a in args) + sum(
        o.size * o.dtype.itemsize for o in outs
    )
    return pl.pallas_call(
        body,
        out_shape=outs,
        in_specs=[pl.BlockSpec(memory_space=space) for space in spaces],
        out_specs=[pl.BlockSpec(memory_space=space) for space in out_spaces],
        input_output_aliases=aliases or {},
        scratch_shapes=list(scratch),
        compiler_params=pltpu.CompilerParams(vmem_limit_bytes=vmem * 2**20),
        cost_estimate=pl.CostEstimate(flops=flops, bytes_accessed=moved, transcendentals=0),
        interpret=INTERPRET,
    )(*args)


def silu(v):
    half = 0.5 * v
    return half + half * jnp.tanh(half)


def split(v):
    hi = v.astype(BF16)
    return hi, (v - hi.astype(F32)).astype(BF16)


def iota(shape, dim):
    return lax.broadcasted_iota(jnp.int32, shape, dim)


def as_column(row):
    heads = row.shape[1]
    same = iota((PAD_HEADS, heads), 0) == iota((PAD_HEADS, heads), 1)
    return jnp.sum(jnp.where(same, row, 0.0), axis=1, keepdims=True)


def head_spread(width, dtype):
    return (iota((PAD_HEADS, width), 1) // HEADDIM == iota((PAD_HEADS, width), 0)).astype(dtype)


def spread_tokens(per_head, spread2):
    hi, lo = split(per_head)
    return dot(jnp.concatenate([hi, lo], axis=0), spread2, TN)


def spread_row(column, spread_f32):
    return jnp.sum(spread_f32 * column, axis=0, keepdims=True)


def fetch(sems, *pairs):
    copies = [pltpu.make_async_copy(a, b, sems.at[i]) for i, (a, b) in enumerate(pairs)]
    for copy in copies:
        copy.start()
    return copies


def conv_silu(padded, taps_ref, at, rows):
    first = 8 - (CONV - 1) + at
    total = taps_ref[0:1, :] * padded[first : first + rows, :]
    for k in range(1, CONV):
        total += taps_ref[k : k + 1, :] * padded[first + k : first + k + rows, :]
    return silu(total).astype(BF16)


def front_kernel(
    x_hbm, bc_hbm, dt_hbm, tap_x_hbm, tap_bc_hbm, bias_hbm, alog_hbm,
    xc_ref, bcc_ref, cum_ref, logstep_ref, state_ref, tail_ref,
    x_ref, bc_ref, dt_ref, tap_x_ref, tap_bc_ref, bias_ref, alog_ref,
    x_scr, bc_scr, logit_scr, fed_scr, sems,
):
    copies = fetch(
        sems, (dt_hbm, dt_ref), (bias_hbm, bias_ref), (alog_hbm, alog_ref), (bc_hbm, bc_ref),
        (tap_bc_hbm, tap_bc_ref), (tap_x_hbm, tap_x_ref), (x_hbm, x_ref),
    )
    tokens, width = x_ref.shape
    heads = dt_ref.shape[0]
    for copy in copies[:3]:
        copy.wait()
    logit_scr[...] = jnp.zeros_like(logit_scr)
    logit_scr[0:heads, :] = dt_ref[...].astype(F32)
    logits = logit_scr[...] + as_column(bias_ref[...])
    small = jnp.exp(-jnp.abs(logits))
    series = small * (1.0 - small * (0.5 - small * (1.0 / 3.0 - small * 0.25)))
    step = jnp.maximum(logits, 0.0) + jnp.where(small < 0.015625, series, jnp.log(1.0 + small))
    logstep = jnp.log(step)
    rate = -jnp.exp(as_column(alog_ref[...])) * step
    upto = (iota((CHUNK, CHUNK), 0) <= iota((CHUNK, CHUNK), 1)).astype(F32)
    run = jnp.zeros((PAD_HEADS, 1), F32)
    sums = []
    for at in range(0, tokens, CHUNK):
        within = dot(rate[:, at : at + CHUNK], upto, precision=HIGH) + run
        run = within[:, CHUNK - 1 :]
        sums.append(within)
    cum = jnp.concatenate(sums, axis=1)
    cum_ref[...] = cum
    logstep_ref[...] = logstep
    spread = head_spread(width, BF16)
    tail = spread_tokens(jnp.exp(run - cum + logstep), jnp.concatenate([spread, spread], axis=0))
    tail_ref[...] = tail[:RIM, :]

    for copy in copies[3:]:
        copy.wait()
    bc_scr[0:8, :] = jnp.zeros((8, bc_scr.shape[1]), F32)
    bc_scr[8:, :] = bc_ref[...].astype(F32)
    x_scr[0:8, :] = jnp.zeros((8, width), F32)
    x_scr[8:, :] = x_ref[...].astype(F32)
    for at in range(0, tokens, CHUNK):
        rows = slice(at, at + CHUNK)
        bcc_ref[rows, :] = conv_silu(bc_scr, tap_bc_ref, at, CHUNK)
        xc = conv_silu(x_scr, tap_x_ref, at, CHUNK)
        xc_ref[rows, :] = xc
        fed_scr[rows, :] = (xc.astype(F32) * tail[rows, :]).astype(BF16)
    fed_scr[0:RIM, :] = jnp.zeros((RIM, width), BF16)
    state_ref[...] = dot(bcc_ref[:, :STATE], fed_scr[...], TN)


def pack_decay(total, width):
    spread = head_spread(width, F32)
    hi, lo = split(total)
    even = iota((1, width), 1) % 2 == 0
    return jnp.where(even, spread_row(hi.astype(F32), spread), spread_row(lo.astype(F32), spread))


def rim_kernel(
    rim_ref, x_hbm, bc_hbm, tap_x_hbm, tap_bc_hbm, cum_ref, tail_ref, state_ref,
    xc_ref, bcc_ref, piece_ref, x_ref, bc_ref, tap_x_ref, tap_bc_ref, x_scr, bc_scr, piece_scr, sems,
):
    copies = fetch(
        sems, (x_hbm.at[0:RIM, :], x_ref), (bc_hbm.at[0:RIM, :], bc_ref),
        (tap_x_hbm, tap_x_ref), (tap_bc_hbm, tap_bc_ref),
    )
    width = x_ref.shape[1]
    rim = rim_ref[...].astype(F32)
    x_scr[0:8, :] = rim[RIM - 8 :, :width]
    bc_scr[0:8, :] = rim[RIM - 8 :, width:]
    last = cum_ref.shape[1] - 1
    decay = pack_decay(cum_ref[:, last:], width)
    for copy in copies:
        copy.wait()
    x_scr[8:, :] = x_ref[...].astype(F32)
    bc_scr[8:, :] = bc_ref[...].astype(F32)
    xc = conv_silu(x_scr, tap_x_ref, 0, RIM)
    bcc = conv_silu(bc_scr, tap_bc_ref, 0, RIM)
    xc_ref[...] = xc
    bcc_ref[...] = bcc
    fed = (xc.astype(F32) * tail_ref[...]).astype(BF16)
    state = state_ref[...] + dot(bcc[:, :STATE], fed, TN)
    each = STATE // Z_RING
    blocks = width // LANES
    for j in range(Z_RING):
        for b in range(blocks):
            at = j * PIECE + b * each
            piece_scr[at : at + each, :] = state[
                j * each : (j + 1) * each, b * LANES : (b + 1) * LANES
            ]
        at = j * PIECE + blocks * each
        piece_scr[at : at + 8, :] = jnp.zeros((8, LANES), F32)
        for b in range(blocks):
            piece_scr[at + b : at + b + 1, :] = decay[:, b * LANES : (b + 1) * LANES]
    piece_ref[...] = piece_scr[...].astype(BF16)


def local_kernel(
    xc_ref, xc_rim_ref, bcc_ref, bcc_rim_ref, cum_ref, logstep_ref, z_hbm, skip_hbm,
    own_ref, reach_ref, c_ref, held, xs, bs, z_ref, skip_ref, sems,
):
    copies = fetch(sems, (skip_hbm, skip_ref), (z_hbm, z_ref))
    tokens, width = xc_ref.shape
    xs[...] = xc_ref[...]
    xs[0:RIM, :] = xc_rim_ref[...]
    bs[...] = bcc_ref[...]
    bs[0:RIM, :] = bcc_rim_ref[...]
    c_ref[...] = bs[:, STATE:]
    spread = head_spread(width, BF16)
    spread2 = jnp.concatenate([spread, spread], axis=0)
    spread_f = head_spread(width, F32)
    causal = iota((CHUNK, CHUNK), 0) >= iota((CHUNK, CHUNK), 1)
    left = iota((CHUNK, LANES), 1) < HEADDIM
    held[...] = jnp.zeros_like(held)
    before = jnp.zeros((PAD_HEADS, 1), F32)
    for copy in copies:
        copy.wait()
    skip = spread_row(as_column(skip_ref[...]), spread_f)
    for at in range(0, tokens, CHUNK):
        rows = slice(at, at + CHUNK)
        b_part, c_part = bs[rows, :STATE], bs[rows, STATE:]
        cum = cum_ref[:, rows]
        source = logstep_ref[:, rows] - cum
        cum_cols = cum.T
        last = cum[:, CHUNK - 1 :]
        cb = dot(c_part, b_part, NT)
        gate = silu(z_ref[rows, :].astype(F32))
        reach_ref[rows, :] = spread_tokens(jnp.exp(cum), spread2) * gate
        fresh = spread_tokens(jnp.exp(cum - before), spread2)
        carried = dot(c_part, held[...].astype(BF16)) * fresh
        for pair in range(width // LANES):
            cols = slice(pair * LANES, (pair + 1) * LANES)
            mixes = []
            for head in (2 * pair, 2 * pair + 1):
                power = cum_cols[:, head : head + 1] + source[head : head + 1, :]
                mixes.append((cb * jnp.exp(jnp.where(causal, power, MASKED))).astype(BF16))
            x_part = xs[rows, cols]
            blank = jnp.zeros_like(x_part)
            x_two = jnp.concatenate(
                [jnp.where(left, x_part, blank), jnp.where(left, blank, x_part)], axis=0
            )
            y = dot(jnp.concatenate(mixes, axis=1), x_two) + carried[:, cols]
            y += skip[:, cols] * x_part.astype(F32)
            own_ref[rows, cols] = y * gate[:, cols]
        if at + CHUNK < tokens:
            tail = spread_tokens(jnp.exp(last + source), spread2)
            fed = (xs[rows, :].astype(F32) * tail).astype(BF16)
            kept = spread_row(jnp.exp(last - before), spread_f)
            held[...] = held[...] * kept + dot(b_part, fed, TN)
            before = last


def decay_rows(wide, at):
    both = wide[at : at + 8, :]
    even = iota((8, LANES), 1) % 2 == 0
    return both + jnp.where(even, pltpu.roll(both, LANES - 1, 1), pltpu.roll(both, 1, 1))


def total_kernel(blocks, in_ref, out_ref, wide):
    wide[...] = in_ref[...].astype(F32)
    carry = [jnp.zeros((8, LANES), F32)] * blocks
    passed = jnp.zeros((8, LANES), F32)
    for place in range(Z_RING):
        at = place * PIECE
        logs = decay_rows(wide, at + 8 * blocks)
        passed += logs
        kept = jnp.exp(logs)
        carry = [
            kept[b : b + 1, :] * carry[b] + wide[at + 8 * b : at + 8 * b + 8, :]
            for b in range(blocks)
        ]
    for peer in range(out_ref.shape[0]):
        for b in range(blocks):
            out_ref[peer, 8 * b : 8 * b + 8, :] = carry[b]
        out_ref[peer, 8 * blocks : 8 * blocks + 8, :] = passed


def scan_kernel(blocks, in_ref, total_ref, place_ref, out_ref, wide):
    wide[...] = in_ref[...].astype(F32)
    carry = [jnp.zeros((8, LANES), F32)] * blocks
    for peer in range(total_ref.shape[0] - 1):
        earlier = peer < place_ref[0, 0]
        kept = jnp.exp(total_ref[peer, 8 * blocks : 8 * blocks + 8, :])
        carry = [
            jnp.where(
                earlier,
                kept[b : b + 1, :] * carry[b] + total_ref[peer, 8 * b : 8 * b + 8, :],
                carry[b],
            )
            for b in range(blocks)
        ]
    for place in range(Z_RING):
        at = place * PIECE
        kept = jnp.exp(decay_rows(wide, at + 8 * blocks))
        for b in range(blocks):
            part = wide[at + 8 * b : at + 8 * b + 8, :]
            wide[at + 8 * b : at + 8 * b + 8, :] = carry[b]
            carry[b] = kept[b : b + 1, :] * carry[b] + part
    out_ref[...] = wide[...].astype(BF16)


def rim_source_kernel(x_hbm, bc_hbm, out_ref, sems):
    tokens, width = x_hbm.shape
    for copy in fetch(
        sems,
        (x_hbm.at[tokens - RIM :, :], out_ref.at[:, 0:width]),
        (bc_hbm.at[tokens - RIM :, :], out_ref.at[:, width:]),
    ):
        copy.wait()


def fetch_half(w_hbm, w_ref, half, sems):
    parts = w_ref.shape[0] // (TARGETS // 2 * Z_STRIDE)
    return fetch(
        sems,
        *[
            (
                w_hbm.at[pl.ds(pl.multiple_of((2 * k + half) * parts, parts), parts), :],
                w_ref.at[k * parts : (k + 1) * parts, :],
            )
            for k in range(TARGETS // 2 * Z_STRIDE)
        ],
    )


def back_kernel(
    own_ref, reach_ref, c_ref, piece_ref, w_hbm, gain_ref, place_ref,
    out_ref, gated_ref, square_ref, wide, state, w_ref, sems,
):
    copies = fetch_half(w_hbm, w_ref, 1 - place_ref[0, 1] % 2, sems)
    tokens, width = own_ref.shape
    blocks = width // LANES
    each = STATE // Z_RING
    wide[...] = piece_ref[...].astype(F32)
    for j in range(Z_RING):
        for b in range(blocks):
            at = j * PIECE + b * each
            state[j * each : (j + 1) * each, b * LANES : (b + 1) * LANES] = wide[at : at + each, :]
    incoming = state[...].astype(BF16)
    ones = jnp.ones((16, 2 * width), BF16)
    totals = []
    for at in range(0, tokens, CHUNK):
        rows = slice(at, at + CHUNK)
        y = own_ref[rows, :] + reach_ref[rows, :] * dot(c_ref[rows, :], incoming)
        gated_ref[rows, :] = (y * gain_ref[...]).astype(BF16)
        hi, lo = split(y * y)
        totals.append(dot(ones, jnp.concatenate([hi, lo], axis=1), NT))
    hi, lo = split(jnp.concatenate(totals, axis=1))
    row = iota((16, tokens), 0)
    mine = 2 * place_ref[0, 1]
    zero = jnp.zeros((16, tokens), F32)
    squares = jnp.where(
        row == mine, hi.astype(F32), jnp.where(row == mine + 1, lo.astype(F32), zero)
    ).astype(BF16)
    square_ref[...] = squares
    for copy in copies:
        copy.wait()
    block = w_ref.shape[0] // (TARGETS // 2)
    for y in range(TARGETS // 2):
        to = y * (block + 16)
        out_ref[to : to + block, :] = dot(
            w_ref[y * block : (y + 1) * block, :], gated_ref[...], NT
        ).astype(BF16)
        out_ref[to + block : to + block + 16, :] = squares


def kept_kernel(gated_ref, w_hbm, place_ref, out_ref, w_ref, sems):
    copies = fetch_half(w_hbm, w_ref, place_ref[0, 1] % 2, sems)
    block = w_ref.shape[0] // (TARGETS // 2)
    for y in range(TARGETS // 2):
        rows = slice(y * block, (y + 1) * block)
        for copy in copies[y * Z_STRIDE : (y + 1) * Z_STRIDE]:
            copy.wait()
        out_ref[rows, :] = dot(w_ref[rows, :], gated_ref[...], NT).astype(BF16)


def pair_kernel(kept_ref, got_ref, square_ref, out_ref):
    block = kept_ref.shape[0] // (TARGETS // 2)
    for y in range(TARGETS // 2):
        to = y * (block + 16)
        rows = slice(to, to + block)
        out_ref[rows, :] = (
            kept_ref[y * block : (y + 1) * block, :].astype(F32) + got_ref[rows, :].astype(F32)
        ).astype(BF16)
        rows = slice(to + block, to + block + 16)
        out_ref[rows, :] = (square_ref[...].astype(F32) + got_ref[rows, :].astype(F32)).astype(BF16)


def scale_kernel(in_ref, out_ref):
    block = out_ref.shape[0]
    parts = TARGETS // 2
    each = block + 16
    total = jnp.zeros((1, out_ref.shape[1]), F32)
    for y in range(parts):
        part = in_ref[y * each + block : (y + 1) * each, :].astype(F32)
        total += jnp.sum(part, axis=0, keepdims=True)
    scale = lax.rsqrt(total / CHANNELS + EPSILON)
    mixed = in_ref[0:block, :].astype(F32)
    for y in range(1, parts):
        mixed += in_ref[y * each : y * each + block, :].astype(F32)
    mixed *= scale
    shard = block // (2 * Z_STRIDE)
    out_ref[...] = jnp.concatenate(
        [
            mixed[(low * 2 + high) * shard : (low * 2 + high + 1) * shard, :]
            for high in range(2)
            for low in range(Z_STRIDE)
        ],
        axis=0,
    ).astype(BF16)


def shaped(shape, dtype):
    return jax.ShapeDtypeStruct(shape, dtype)


def held_like(*arrays):
    return tuple(pltpu.VMEM(a.shape, a.dtype) for a in arrays)


def front(x_in, bc_in, dt_t, conv_x, conv_bc, dt_bias, a_log):
    tokens, width = x_in.shape
    args = (x_in, bc_in, dt_t, conv_x, conv_bc, dt_bias, a_log)
    return call(
        front_kernel,
        [
            shaped((tokens, width), BF16),
            shaped((tokens, 2 * STATE), BF16),
            shaped((PAD_HEADS, tokens), F32),
            shaped((PAD_HEADS, tokens), F32),
            shaped((STATE, width), F32),
            shaped((RIM, width), F32),
        ],
        8 * tokens * width * STATE,
        *args,
        spaces=[pltpu.HBM] * 7,
        vmem=FULL,
        scratch=held_like(*args)
        + (
            pltpu.VMEM((tokens + 8, width), F32),
            pltpu.VMEM((tokens + 8, 2 * STATE), F32),
            pltpu.VMEM((PAD_HEADS, tokens), F32),
            pltpu.VMEM((tokens, width), BF16),
            pltpu.SemaphoreType.DMA((7,)),
        ),
    )


def add_rim(rim, x_in, bc_in, conv_x, conv_bc, cum, tail, state):
    width = x_in.shape[1]
    return call(
        rim_kernel,
        [
            shaped((RIM, width), BF16),
            shaped((RIM, 2 * STATE), BF16),
            shaped((Z_RING * PIECE, LANES), BF16),
        ],
        2 * 128 * width * STATE,
        rim, x_in, bc_in, conv_x, conv_bc, cum, tail, state,
        spaces=[pltpu.VMEM] + [pltpu.HBM] * 4 + [pltpu.VMEM] * 3,
        vmem=FULL,
        scratch=(
            pltpu.VMEM((RIM, width), BF16),
            pltpu.VMEM((RIM, 2 * STATE), BF16),
            *held_like(conv_x, conv_bc),
            pltpu.VMEM((RIM + 8, width), F32),
            pltpu.VMEM((RIM + 8, 2 * STATE), F32),
            pltpu.VMEM((Z_RING * PIECE, LANES), F32),
            pltpu.SemaphoreType.DMA((4,)),
        ),
    )


def local(xc, xc_rim, bcc, bcc_rim, cum, logstep, z_gate, d_skip):
    tokens, width = xc.shape
    return call(
        local_kernel,
        [shaped((tokens, width), F32)] * 2 + [shaped((tokens, STATE), BF16)],
        12 * tokens * width * STATE,
        xc, xc_rim, bcc, bcc_rim, cum, logstep, z_gate, d_skip,
        spaces=[pltpu.VMEM] * 6 + [pltpu.HBM] * 2,
        scratch=(pltpu.VMEM((STATE, width), F32),)
        + held_like(xc, bcc, z_gate, d_skip)
        + (pltpu.SemaphoreType.DMA((2,)),),
    )


def row_total(pieces, width, peers):
    def body(*refs):
        total_kernel(width // LANES, *refs)

    return call(
        body,
        [shaped((peers, PIECE, LANES), F32)],
        pieces.size * 4,
        pieces,
        scratch=(pltpu.VMEM(pieces.shape, F32),),
    )[0]


def scan(pieces, totals, place, width):
    def body(*refs):
        scan_kernel(width // LANES, *refs)

    return call(
        body,
        [shaped(pieces.shape, BF16)],
        pieces.size * 4,
        pieces, totals, place,
        spaces=[pltpu.VMEM, pltpu.VMEM, pltpu.SMEM],
        scratch=(pltpu.VMEM(pieces.shape, F32),),
    )[0]


def rim_source(x_in, bc_in):
    return call(
        rim_source_kernel,
        [shaped((RIM, x_in.shape[1] + bc_in.shape[1]), BF16)],
        0,
        x_in, bc_in,
        spaces=[pltpu.HBM] * 2,
        vmem=FULL,
        scratch=(pltpu.SemaphoreType.DMA((2,)),),
    )[0]


def back(own, reach, c_part, pieces, weight, norm_gain, place):
    tokens, width = own.shape
    columns = weight.shape[0]
    half = columns // 2
    parts = TARGETS // 2
    return call(
        back_kernel,
        [
            shaped((half + parts * 16, tokens), BF16),
            shaped((tokens, width), BF16),
            shaped((16, tokens), BF16),
        ],
        2 * tokens * width * (half + STATE),
        own, reach, c_part, pieces, weight, norm_gain[None], place,
        spaces=[pltpu.VMEM] * 4 + [pltpu.HBM, pltpu.VMEM, pltpu.SMEM],
        vmem=FULL - 5,
        scratch=(
            pltpu.VMEM(pieces.shape, F32),
            pltpu.VMEM((STATE, width), F32),
            pltpu.VMEM((half, width), BF16),
            pltpu.SemaphoreType.DMA((parts * Z_STRIDE,)),
        ),
    )


def kept_part(gated, weight, place):
    tokens, width = gated.shape
    half = weight.shape[0] // 2
    return call(
        kept_kernel,
        [shaped((half, tokens), BF16)],
        2 * tokens * width * half,
        gated, weight, place,
        spaces=[pltpu.VMEM, pltpu.HBM, pltpu.SMEM],
        vmem=FULL - 2,
        scratch=(
            pltpu.VMEM((half, width), BF16),
            pltpu.SemaphoreType.DMA((TARGETS // 2 * Z_STRIDE,)),
        ),
    )[0]


def pair_sum(kept, got, squares):
    return call(pair_kernel, [shaped(got.shape, BF16)], got.size, kept, got, squares)[0]


def scaled(parts):
    rows, tokens = parts.shape
    block = rows // (TARGETS // 2) - 16
    return call(scale_kernel, [shaped((block, tokens), BF16)], rows * tokens, parts)[0]


def on_device(
    x_in, bc_in, z_gate, dt_in, conv_x, conv_bc, dt_bias, a_log, d_skip, norm_gain, out_weight
):
    tokens, width = x_in.shape
    count = lax.axis_size("seq")
    rows = count // Z_RING
    along_z = [[x * Z_RING + z for z in range(Z_RING)] for x in range(rows)]
    along_x = [[x * Z_RING + z for x in range(rows)] for z in range(Z_RING)]
    spans = range(Z_RING // Z_STRIDE)
    far = [[x * Z_RING + h * Z_STRIDE + l for h in spans] for x in range(rows) for l in range(Z_STRIDE)]
    near = [[x * Z_RING + h * Z_STRIDE + l for l in range(Z_STRIDE)] for x in range(rows) for h in spans]
    weight = out_weight.T
    for groups in (far, near, along_x):
        weight = lax.all_gather(weight, "seq", axis=0, tiled=True, axis_index_groups=groups)
    rim = lax.ppermute(rim_source(x_in, bc_in), "seq", [(i, i + 1) for i in range(count - 1)])
    place = jnp.stack(
        [lax.axis_index("seq") // Z_RING, lax.axis_index("tp")]
    ).astype(jnp.int32)[None]

    xc, bcc, cum, logstep, state, tail = front(
        x_in, bc_in, dt_in.T, conv_x, conv_bc, dt_bias[None], a_log[None]
    )
    xc_rim, bcc_rim, pieces = add_rim(rim, x_in, bc_in, conv_x, conv_bc, cum, tail, state)
    pieces = lax.all_to_all(pieces, "seq", 0, 0, tiled=True, axis_index_groups=along_z)
    own, reach, c_part = local(xc, xc_rim, bcc, bcc_rim, cum, logstep, z_gate, d_skip[None])
    totals = row_total(pieces, width, rows)
    totals = lax.all_to_all(totals, "seq", 0, 0, tiled=True, axis_index_groups=along_x)
    pieces = scan(pieces, totals, place, width)
    pieces = lax.all_to_all(pieces, "seq", 0, 0, tiled=True, axis_index_groups=along_z)

    given, gated, squares = back(own, reach, c_part, pieces, weight, norm_gain, place)
    got = lax.ppermute(given, "tp", [(i, i ^ 1) for i in range(TARGETS)])
    kept = kept_part(gated, weight, place)
    parts = pair_sum(kept, got, squares)
    along_y = [[core + 2 * y for y in range(TARGETS // 2)] for core in range(2)]
    parts = lax.all_to_all(parts, "tp", 0, 0, tiled=True, axis_index_groups=along_y)
    return scaled(parts).T


def solution(mesh):
    in_specs = (
        P("seq", "tp"),
        P("seq", None),
        P("seq", "tp"),
        P("seq", "tp"),
        P(None, "tp"),
        P(),
        P("tp"),
        P("tp"),
        P("tp"),
        P("tp"),
        P("tp", "seq"),
    )
    return jax.shard_map(
        on_device, mesh=mesh, in_specs=in_specs, out_specs=P("seq", "tp"), check_vma=False
    )
```

```python
import jax
import jax.numpy as jnp
from jax import lax
from jax.experimental import pallas as pl
from jax.experimental.pallas import tpu as pltpu
from jax.sharding import PartitionSpec as P

CHANNELS = 5120
HEADDIM = 64
STATE = 128
CONV = 4
CHUNK = 128
LANES = 128
RIM = 16
PAD_HEADS = 16
Z_RING = 16
PIECE = 48
TARGETS = 8
FULL = 63
EPSILON = 1e-05
HIGH = lax.Precision.HIGHEST
F32 = jnp.float32
BF16 = jnp.bfloat16
MASKED = -1e30
INTERPRET = False

NT = (((1,), (1,)), ((), ()))
TN = (((0,), (0,)), ((), ()))
NN = (((1,), (0,)), ((), ()))


def dot(a, b, dims=NN, precision=None):
    return lax.dot_general(a, b, dims, precision=precision, preferred_element_type=F32)


def call(
    body, outs, flops, *args, scratch=(), spaces=None, out_spaces=None, aliases=None, vmem=40
):
    spaces = spaces or [pltpu.VMEM] * len(args)
    out_spaces = out_spaces or [pltpu.VMEM] * len(outs)
    moved = sum(a.size * a.dtype.itemsize for a in args) + sum(
        o.size * o.dtype.itemsize for o in outs
    )
    return pl.pallas_call(
        body,
        out_shape=outs,
        in_specs=[pl.BlockSpec(memory_space=space) for space in spaces],
        out_specs=[pl.BlockSpec(memory_space=space) for space in out_spaces],
        input_output_aliases=aliases or {},
        scratch_shapes=list(scratch),
        compiler_params=pltpu.CompilerParams(vmem_limit_bytes=vmem * 2**20),
        cost_estimate=pl.CostEstimate(flops=flops, bytes_accessed=moved, transcendentals=0),
        interpret=INTERPRET,
    )(*args)


def silu(v):
    half = 0.5 * v
    return half + half * jnp.tanh(half)


def split(v):
    hi = v.astype(BF16)
    return hi, (v - hi.astype(F32)).astype(BF16)


def iota(shape, dim):
    return lax.broadcasted_iota(jnp.int32, shape, dim)


def as_column(row):
    heads = row.shape[1]
    same = iota((PAD_HEADS, heads), 0) == iota((PAD_HEADS, heads), 1)
    return jnp.sum(jnp.where(same, row, 0.0), axis=1, keepdims=True)


def head_spread(width, dtype):
    return (iota((PAD_HEADS, width), 1) // HEADDIM == iota((PAD_HEADS, width), 0)).astype(dtype)


def spread_tokens(per_head, spread2):
    hi, lo = split(per_head)
    return dot(jnp.concatenate([hi, lo], axis=0), spread2, TN)


def spread_row(column, spread_f32):
    return jnp.sum(spread_f32 * column, axis=0, keepdims=True)


def fetch(sems, *pairs):
    copies = [pltpu.make_async_copy(a, b, sems.at[i]) for i, (a, b) in enumerate(pairs)]
    for copy in copies:
        copy.start()
    return copies


def conv_silu(padded, taps_ref, at, rows):
    first = 8 - (CONV - 1) + at
    total = taps_ref[0:1, :] * padded[first : first + rows, :]
    for k in range(1, CONV):
        total += taps_ref[k : k + 1, :] * padded[first + k : first + k + rows, :]
    return silu(total).astype(BF16)


def front_kernel(
    x_hbm, bc_hbm, dt_hbm, tap_x_hbm, tap_bc_hbm, bias_hbm, alog_hbm,
    xc_ref, bcc_ref, cum_ref, logstep_ref, state_ref, tail_ref,
    x_ref, bc_ref, dt_ref, tap_x_ref, tap_bc_ref, bias_ref, alog_ref,
    x_scr, bc_scr, logit_scr, fed_scr, sems,
):
    copies = fetch(
        sems, (dt_hbm, dt_ref), (bias_hbm, bias_ref), (alog_hbm, alog_ref), (bc_hbm, bc_ref),
        (tap_bc_hbm, tap_bc_ref), (tap_x_hbm, tap_x_ref), (x_hbm, x_ref),
    )
    tokens, width = x_ref.shape
    heads = dt_ref.shape[0]
    for copy in copies[:3]:
        copy.wait()
    logit_scr[...] = jnp.zeros_like(logit_scr)
    logit_scr[0:heads, :] = dt_ref[...].astype(F32)
    logits = logit_scr[...] + as_column(bias_ref[...])
    small = jnp.exp(-jnp.abs(logits))
    series = small * (1.0 - small * (0.5 - small * (1.0 / 3.0 - small * 0.25)))
    step = jnp.maximum(logits, 0.0) + jnp.where(small < 0.015625, series, jnp.log(1.0 + small))
    logstep = jnp.log(step)
    rate = -jnp.exp(as_column(alog_ref[...])) * step
    upto = (iota((CHUNK, CHUNK), 0) <= iota((CHUNK, CHUNK), 1)).astype(F32)
    run = jnp.zeros((PAD_HEADS, 1), F32)
    sums = []
    for at in range(0, tokens, CHUNK):
        within = dot(rate[:, at : at + CHUNK], upto, precision=HIGH) + run
        run = within[:, CHUNK - 1 :]
        sums.append(within)
    cum = jnp.concatenate(sums, axis=1)
    cum_ref[...] = cum
    logstep_ref[...] = logstep
    spread = head_spread(width, BF16)
    tail = spread_tokens(jnp.exp(run - cum + logstep), jnp.concatenate([spread, spread], axis=0))
    tail_ref[...] = tail[:RIM, :]

    for copy in copies[3:]:
        copy.wait()
    bc_scr[0:8, :] = jnp.zeros((8, bc_scr.shape[1]), F32)
    bc_scr[8:, :] = bc_ref[...].astype(F32)
    x_scr[0:8, :] = jnp.zeros((8, width), F32)
    x_scr[8:, :] = x_ref[...].astype(F32)
    for at in range(0, tokens, CHUNK):
        rows = slice(at, at + CHUNK)
        bcc_ref[rows, :] = conv_silu(bc_scr, tap_bc_ref, at, CHUNK)
        xc = conv_silu(x_scr, tap_x_ref, at, CHUNK)
        xc_ref[rows, :] = xc
        fed_scr[rows, :] = (xc.astype(F32) * tail[rows, :]).astype(BF16)
    fed_scr[0:RIM, :] = jnp.zeros((RIM, width), BF16)
    state_ref[...] = dot(bcc_ref[:, :STATE], fed_scr[...], TN)


def pack_decay(total, width):
    spread = head_spread(width, F32)
    hi, lo = split(total)
    even = iota((1, width), 1) % 2 == 0
    return jnp.where(even, spread_row(hi.astype(F32), spread), spread_row(lo.astype(F32), spread))


def rim_kernel(
    rim_ref, x_hbm, bc_hbm, tap_x_hbm, tap_bc_hbm, cum_ref, tail_ref, state_ref,
    xc_ref, bcc_ref, piece_ref, x_ref, bc_ref, tap_x_ref, tap_bc_ref, x_scr, bc_scr, piece_scr, sems,
):
    copies = fetch(
        sems, (x_hbm.at[0:RIM, :], x_ref), (bc_hbm.at[0:RIM, :], bc_ref),
        (tap_x_hbm, tap_x_ref), (tap_bc_hbm, tap_bc_ref),
    )
    width = x_ref.shape[1]
    rim = rim_ref[...].astype(F32)
    x_scr[0:8, :] = rim[RIM - 8 :, :width]
    bc_scr[0:8, :] = rim[RIM - 8 :, width:]
    last = cum_ref.shape[1] - 1
    decay = pack_decay(cum_ref[:, last:], width)
    for copy in copies:
        copy.wait()
    x_scr[8:, :] = x_ref[...].astype(F32)
    bc_scr[8:, :] = bc_ref[...].astype(F32)
    xc = conv_silu(x_scr, tap_x_ref, 0, RIM)
    bcc = conv_silu(bc_scr, tap_bc_ref, 0, RIM)
    xc_ref[...] = xc
    bcc_ref[...] = bcc
    fed = (xc.astype(F32) * tail_ref[...]).astype(BF16)
    state = state_ref[...] + dot(bcc[:, :STATE], fed, TN)
    each = STATE // Z_RING
    blocks = width // LANES
    for j in range(Z_RING):
        for b in range(blocks):
            at = j * PIECE + b * each
            piece_scr[at : at + each, :] = state[
                j * each : (j + 1) * each, b * LANES : (b + 1) * LANES
            ]
        at = j * PIECE + blocks * each
        piece_scr[at : at + 8, :] = jnp.zeros((8, LANES), F32)
        for b in range(blocks):
            piece_scr[at + b : at + b + 1, :] = decay[:, b * LANES : (b + 1) * LANES]
    piece_ref[...] = piece_scr[...].astype(BF16)


def local_kernel(
    xc_ref, xc_rim_ref, bcc_ref, bcc_rim_ref, cum_ref, logstep_ref, z_hbm, skip_hbm,
    own_ref, reach_ref, c_ref, held, xs, bs, z_ref, skip_ref, sems,
):
    copies = fetch(sems, (skip_hbm, skip_ref), (z_hbm, z_ref))
    tokens, width = xc_ref.shape
    xs[...] = xc_ref[...]
    xs[0:RIM, :] = xc_rim_ref[...]
    bs[...] = bcc_ref[...]
    bs[0:RIM, :] = bcc_rim_ref[...]
    c_ref[...] = bs[:, STATE:]
    spread = head_spread(width, BF16)
    spread2 = jnp.concatenate([spread, spread], axis=0)
    spread_f = head_spread(width, F32)
    causal = iota((CHUNK, CHUNK), 0) >= iota((CHUNK, CHUNK), 1)
    left = iota((CHUNK, LANES), 1) < HEADDIM
    held[...] = jnp.zeros_like(held)
    before = jnp.zeros((PAD_HEADS, 1), F32)
    for copy in copies:
        copy.wait()
    skip = spread_row(as_column(skip_ref[...]), spread_f)
    for at in range(0, tokens, CHUNK):
        rows = slice(at, at + CHUNK)
        b_part, c_part = bs[rows, :STATE], bs[rows, STATE:]
        cum = cum_ref[:, rows]
        source = logstep_ref[:, rows] - cum
        cum_cols = cum.T
        last = cum[:, CHUNK - 1 :]
        cb = dot(c_part, b_part, NT)
        gate = silu(z_ref[rows, :].astype(F32))
        reach_ref[rows, :] = spread_tokens(jnp.exp(cum), spread2) * gate
        fresh = spread_tokens(jnp.exp(cum - before), spread2)
        carried = dot(c_part, held[...].astype(BF16)) * fresh
        for pair in range(width // LANES):
            cols = slice(pair * LANES, (pair + 1) * LANES)
            mixes = []
            for head in (2 * pair, 2 * pair + 1):
                power = cum_cols[:, head : head + 1] + source[head : head + 1, :]
                mixes.append((cb * jnp.exp(jnp.where(causal, power, MASKED))).astype(BF16))
            x_part = xs[rows, cols]
            blank = jnp.zeros_like(x_part)
            x_two = jnp.concatenate(
                [jnp.where(left, x_part, blank), jnp.where(left, blank, x_part)], axis=0
            )
            y = dot(jnp.concatenate(mixes, axis=1), x_two) + carried[:, cols]
            y += skip[:, cols] * x_part.astype(F32)
            own_ref[rows, cols] = y * gate[:, cols]
        if at + CHUNK < tokens:
            tail = spread_tokens(jnp.exp(last + source), spread2)
            fed = (xs[rows, :].astype(F32) * tail).astype(BF16)
            kept = spread_row(jnp.exp(last - before), spread_f)
            held[...] = held[...] * kept + dot(b_part, fed, TN)
            before = last


def decay_rows(wide, at):
    both = wide[at : at + 8, :]
    even = iota((8, LANES), 1) % 2 == 0
    return both + jnp.where(even, pltpu.roll(both, LANES - 1, 1), pltpu.roll(both, 1, 1))


def total_kernel(blocks, in_ref, out_ref, wide):
    wide[...] = in_ref[...].astype(F32)
    carry = [jnp.zeros((8, LANES), F32)] * blocks
    passed = jnp.zeros((8, LANES), F32)
    for place in range(Z_RING):
        at = place * PIECE
        logs = decay_rows(wide, at + 8 * blocks)
        passed += logs
        kept = jnp.exp(logs)
        carry = [
            kept[b : b + 1, :] * carry[b] + wide[at + 8 * b : at + 8 * b + 8, :]
            for b in range(blocks)
        ]
    for peer in range(out_ref.shape[0]):
        for b in range(blocks):
            out_ref[peer, 8 * b : 8 * b + 8, :] = carry[b]
        out_ref[peer, 8 * blocks : 8 * blocks + 8, :] = passed


def scan_kernel(blocks, in_ref, total_ref, place_ref, out_ref, wide):
    wide[...] = in_ref[...].astype(F32)
    carry = [jnp.zeros((8, LANES), F32)] * blocks
    for peer in range(total_ref.shape[0] - 1):
        earlier = peer < place_ref[0, 0]
        kept = jnp.exp(total_ref[peer, 8 * blocks : 8 * blocks + 8, :])
        carry = [
            jnp.where(
                earlier,
                kept[b : b + 1, :] * carry[b] + total_ref[peer, 8 * b : 8 * b + 8, :],
                carry[b],
            )
            for b in range(blocks)
        ]
    for place in range(Z_RING):
        at = place * PIECE
        kept = jnp.exp(decay_rows(wide, at + 8 * blocks))
        for b in range(blocks):
            part = wide[at + 8 * b : at + 8 * b + 8, :]
            wide[at + 8 * b : at + 8 * b + 8, :] = carry[b]
            carry[b] = kept[b : b + 1, :] * carry[b] + part
    out_ref[...] = wide[...].astype(BF16)


def rim_source_kernel(x_hbm, bc_hbm, out_ref, sems):
    tokens, width = x_hbm.shape
    for copy in fetch(
        sems,
        (x_hbm.at[tokens - RIM :, :], out_ref.at[:, 0:width]),
        (bc_hbm.at[tokens - RIM :, :], out_ref.at[:, width:]),
    ):
        copy.wait()


def gate_kernel(
    own_ref, reach_ref, c_ref, piece_ref, gain_ref, place_ref, gated_ref, square_ref, wide, state,
):
    tokens, width = own_ref.shape
    blocks = width // LANES
    each = STATE // Z_RING
    wide[...] = piece_ref[...].astype(F32)
    for j in range(Z_RING):
        for b in range(blocks):
            at = j * PIECE + b * each
            state[j * each : (j + 1) * each, b * LANES : (b + 1) * LANES] = wide[at : at + each, :]
    incoming = state[...].astype(BF16)
    ones = jnp.ones((16, 2 * width), BF16)
    totals = []
    for at in range(0, tokens, CHUNK):
        rows = slice(at, at + CHUNK)
        y = own_ref[rows, :] + reach_ref[rows, :] * dot(c_ref[rows, :], incoming)
        gated_ref[rows, :] = (y * gain_ref[...]).astype(BF16)
        hi, lo = split(y * y)
        totals.append(dot(ones, jnp.concatenate([hi, lo], axis=1), NT))
    hi, lo = split(jnp.concatenate(totals, axis=1))
    row = iota((16, tokens), 0)
    mine = 2 * place_ref[0, 1]
    zero = jnp.zeros((16, tokens), F32)
    square_ref[...] = jnp.where(
        row == mine, hi.astype(F32), jnp.where(row == mine + 1, lo.astype(F32), zero)
    ).astype(BF16)


def project_half(w_hbm, gated, half, out_ref, w_ref, acc, sems, gap):
    span = w_ref.shape[0]
    parts = 2
    step = span // parts
    copies = fetch(
        sems,
        *[
            (
                w_hbm.at[pl.ds(pl.multiple_of(half * span + k * step, step), step), :],
                w_ref.at[k * step : (k + 1) * step, :],
            )
            for k in range(parts)
        ],
    )
    for k, copy in enumerate(copies):
        rows = slice(k * step, (k + 1) * step)
        copy.wait()
        acc[rows, :] = dot(w_ref[rows, :], gated, NT)
    block = span // (TARGETS // 2)
    shard = block // (Z_RING // 2)
    for x in range(TARGETS // 2):
        to = x * (block + gap)
        out_ref[to : to + block, :] = jnp.concatenate(
            [
                acc[z * block // 2 + x * shard : z * block // 2 + (x + 1) * shard, :]
                for z in range(Z_RING // 2)
            ],
            axis=0,
        ).astype(BF16)


def given_kernel(gated_ref, square_ref, w_hbm, place_ref, out_ref, w_ref, acc, sems):
    half = 1 - place_ref[0, 1] % 2
    project_half(w_hbm, gated_ref[...], half, out_ref, w_ref, acc, sems, 16)
    each = out_ref.shape[0] // (TARGETS // 2)
    for x in range(TARGETS // 2):
        out_ref[(x + 1) * each - 16 : (x + 1) * each, :] = square_ref[...]


def kept_kernel(gated_ref, w_hbm, place_ref, out_ref, w_ref, acc, sems):
    project_half(w_hbm, gated_ref[...], place_ref[0, 1] % 2, out_ref, w_ref, acc, sems, 0)


def pair_kernel(kept_ref, got_ref, square_ref, out_ref):
    block = kept_ref.shape[0] // (TARGETS // 2)
    for y in range(TARGETS // 2):
        to = y * (block + 16)
        rows = slice(to, to + block)
        out_ref[rows, :] = (
            kept_ref[y * block : (y + 1) * block, :].astype(F32) + got_ref[rows, :].astype(F32)
        ).astype(BF16)
        rows = slice(to + block, to + block + 16)
        out_ref[rows, :] = (square_ref[...].astype(F32) + got_ref[rows, :].astype(F32)).astype(BF16)


def scale_kernel(in_ref, out_ref):
    block = out_ref.shape[0]
    parts = TARGETS // 2
    each = block + 16
    total = jnp.zeros((1, out_ref.shape[1]), F32)
    for y in range(parts):
        part = in_ref[y * each + block : (y + 1) * each, :].astype(F32)
        total += jnp.sum(part, axis=0, keepdims=True)
    scale = lax.rsqrt(total / CHANNELS + EPSILON)
    mixed = in_ref[0:block, :].astype(F32)
    for y in range(1, parts):
        mixed += in_ref[y * each : y * each + block, :].astype(F32)
    out_ref[...] = (mixed * scale).astype(BF16)


def shaped(shape, dtype):
    return jax.ShapeDtypeStruct(shape, dtype)


def held_like(*arrays):
    return tuple(pltpu.VMEM(a.shape, a.dtype) for a in arrays)


def front(x_in, bc_in, dt_t, conv_x, conv_bc, dt_bias, a_log):
    tokens, width = x_in.shape
    args = (x_in, bc_in, dt_t, conv_x, conv_bc, dt_bias, a_log)
    return call(
        front_kernel,
        [
            shaped((tokens, width), BF16),
            shaped((tokens, 2 * STATE), BF16),
            shaped((PAD_HEADS, tokens), F32),
            shaped((PAD_HEADS, tokens), F32),
            shaped((STATE, width), F32),
            shaped((RIM, width), F32),
        ],
        8 * tokens * width * STATE,
        *args,
        spaces=[pltpu.HBM] * 7,
        vmem=FULL,
        scratch=held_like(*args)
        + (
            pltpu.VMEM((tokens + 8, width), F32),
            pltpu.VMEM((tokens + 8, 2 * STATE), F32),
            pltpu.VMEM((PAD_HEADS, tokens), F32),
            pltpu.VMEM((tokens, width), BF16),
            pltpu.SemaphoreType.DMA((7,)),
        ),
    )


def add_rim(rim, x_in, bc_in, conv_x, conv_bc, cum, tail, state):
    width = x_in.shape[1]
    return call(
        rim_kernel,
        [
            shaped((RIM, width), BF16),
            shaped((RIM, 2 * STATE), BF16),
            shaped((Z_RING * PIECE, LANES), BF16),
        ],
        2 * 128 * width * STATE,
        rim, x_in, bc_in, conv_x, conv_bc, cum, tail, state,
        spaces=[pltpu.VMEM] + [pltpu.HBM] * 4 + [pltpu.VMEM] * 3,
        vmem=FULL,
        scratch=(
            pltpu.VMEM((RIM, width), BF16),
            pltpu.VMEM((RIM, 2 * STATE), BF16),
            *held_like(conv_x, conv_bc),
            pltpu.VMEM((RIM + 8, width), F32),
            pltpu.VMEM((RIM + 8, 2 * STATE), F32),
            pltpu.VMEM((Z_RING * PIECE, LANES), F32),
            pltpu.SemaphoreType.DMA((4,)),
        ),
    )


def local(xc, xc_rim, bcc, bcc_rim, cum, logstep, z_gate, d_skip):
    tokens, width = xc.shape
    return call(
        local_kernel,
        [shaped((tokens, width), F32)] * 2 + [shaped((tokens, STATE), BF16)],
        12 * tokens * width * STATE,
        xc, xc_rim, bcc, bcc_rim, cum, logstep, z_gate, d_skip,
        spaces=[pltpu.VMEM] * 6 + [pltpu.HBM] * 2,
        scratch=(pltpu.VMEM((STATE, width), F32),)
        + held_like(xc, bcc, z_gate, d_skip)
        + (pltpu.SemaphoreType.DMA((2,)),),
    )


def row_total(pieces, width, peers):
    def body(*refs):
        total_kernel(width // LANES, *refs)

    return call(
        body,
        [shaped((peers, PIECE, LANES), F32)],
        pieces.size * 4,
        pieces,
        scratch=(pltpu.VMEM(pieces.shape, F32),),
    )[0]


def scan(pieces, totals, place, width):
    def body(*refs):
        scan_kernel(width // LANES, *refs)

    return call(
        body,
        [shaped(pieces.shape, BF16)],
        pieces.size * 4,
        pieces, totals, place,
        spaces=[pltpu.VMEM, pltpu.VMEM, pltpu.SMEM],
        scratch=(pltpu.VMEM(pieces.shape, F32),),
    )[0]


def rim_source(x_in, bc_in):
    return call(
        rim_source_kernel,
        [shaped((RIM, x_in.shape[1] + bc_in.shape[1]), BF16)],
        0,
        x_in, bc_in,
        spaces=[pltpu.HBM] * 2,
        vmem=FULL,
        scratch=(pltpu.SemaphoreType.DMA((2,)),),
    )[0]


def gate(own, reach, c_part, pieces, norm_gain, place):
    tokens, width = own.shape
    return call(
        gate_kernel,
        [shaped((tokens, width), BF16), shaped((16, tokens), BF16)],
        2 * tokens * width * STATE,
        own, reach, c_part, pieces, norm_gain[None], place,
        spaces=[pltpu.VMEM] * 5 + [pltpu.SMEM],
        scratch=(pltpu.VMEM(pieces.shape, F32), pltpu.VMEM((STATE, width), F32)),
    )


def half_scratch(weight, tokens):
    columns, width = weight.shape
    return (
        pltpu.VMEM((columns // 2, width), BF16),
        pltpu.VMEM((columns // 2, tokens), F32),
        pltpu.SemaphoreType.DMA((2,)),
    )


def given_part(gated, squares, weight, place):
    tokens, width = gated.shape
    half = weight.shape[0] // 2
    return call(
        given_kernel,
        [shaped((half + TARGETS // 2 * 16, tokens), BF16)],
        2 * tokens * width * half,
        gated, squares, weight, place,
        spaces=[pltpu.VMEM, pltpu.VMEM, pltpu.HBM, pltpu.SMEM],
        vmem=FULL - 3,
        scratch=half_scratch(weight, tokens),
    )[0]


def kept_part(gated, weight, place):
    tokens, width = gated.shape
    half = weight.shape[0] // 2
    return call(
        kept_kernel,
        [shaped((half, tokens), BF16)],
        2 * tokens * width * half,
        gated, weight, place,
        spaces=[pltpu.VMEM, pltpu.HBM, pltpu.SMEM],
        vmem=FULL - 3,
        scratch=half_scratch(weight, tokens),
    )[0]


def pair_sum(kept, got, squares):
    return call(pair_kernel, [shaped(got.shape, BF16)], got.size, kept, got, squares)[0]


def scaled(parts):
    rows, tokens = parts.shape
    block = rows // (TARGETS // 2) - 16
    return call(scale_kernel, [shaped((block, tokens), BF16)], rows * tokens, parts)[0]


def on_device(
    x_in, bc_in, z_gate, dt_in, conv_x, conv_bc, dt_bias, a_log, d_skip, norm_gain, out_weight
):
    tokens, width = x_in.shape
    count = lax.axis_size("seq")
    rows = count // Z_RING
    along_z = [[x * Z_RING + z for z in range(Z_RING)] for x in range(rows)]
    along_x = [[x * Z_RING + z for x in range(rows)] for z in range(Z_RING)]
    weight = out_weight.T
    for groups in (along_x, along_z):
        weight = lax.all_gather(weight, "seq", axis=0, tiled=True, axis_index_groups=groups)
    rim = lax.ppermute(rim_source(x_in, bc_in), "seq", [(i, i + 1) for i in range(count - 1)])
    place = jnp.stack(
        [lax.axis_index("seq") // Z_RING, lax.axis_index("tp")]
    ).astype(jnp.int32)[None]

    xc, bcc, cum, logstep, state, tail = front(
        x_in, bc_in, dt_in.T, conv_x, conv_bc, dt_bias[None], a_log[None]
    )
    xc_rim, bcc_rim, pieces = add_rim(rim, x_in, bc_in, conv_x, conv_bc, cum, tail, state)
    pieces = lax.all_to_all(pieces, "seq", 0, 0, tiled=True, axis_index_groups=along_z)
    own, reach, c_part = local(xc, xc_rim, bcc, bcc_rim, cum, logstep, z_gate, d_skip[None])
    totals = row_total(pieces, width, rows)
    totals = lax.all_to_all(totals, "seq", 0, 0, tiled=True, axis_index_groups=along_x)
    pieces = scan(pieces, totals, place, width)
    pieces = lax.all_to_all(pieces, "seq", 0, 0, tiled=True, axis_index_groups=along_z)

    gated, squares = gate(own, reach, c_part, pieces, norm_gain, place)
    given = given_part(gated, squares, weight, place)
    got = lax.ppermute(given, "tp", [(i, i ^ 1) for i in range(TARGETS)])
    kept = kept_part(gated, weight, place)
    parts = pair_sum(kept, got, squares)
    along_y = [[core + 2 * y for y in range(TARGETS // 2)] for core in range(2)]
    parts = lax.all_to_all(parts, "tp", 0, 0, tiled=True, axis_index_groups=along_y)
    return scaled(parts).T


def solution(mesh):
    in_specs = (
        P("seq", "tp"),
        P("seq", None),
        P("seq", "tp"),
        P("seq", "tp"),
        P(None, "tp"),
        P(),
        P("tp"),
        P("tp"),
        P("tp"),
        P("tp"),
        P("tp", "seq"),
    )
    return jax.shard_map(
        on_device, mesh=mesh, in_specs=in_specs, out_specs=P("seq", "tp"), check_vma=False
    )
```

```python
import jax
import jax.numpy as jnp
from jax import lax
from jax.experimental import pallas as pl
from jax.experimental.pallas import tpu as pltpu
from jax.sharding import PartitionSpec as P

CHANNELS = 5120
HEADDIM = 64
STATE = 128
CONV = 4
CHUNK = 128
LANES = 128
RIM = 16
PAD_HEADS = 16
Z_RING = 16
PIECE = 48
TARGETS = 8
FULL = 63
EPSILON = 1e-05
HIGH = lax.Precision.HIGHEST
F32 = jnp.float32
BF16 = jnp.bfloat16
MASKED = -1e30
INTERPRET = False

NT = (((1,), (1,)), ((), ()))
TN = (((0,), (0,)), ((), ()))
NN = (((1,), (0,)), ((), ()))


def dot(a, b, dims=NN, precision=None):
    return lax.dot_general(a, b, dims, precision=precision, preferred_element_type=F32)


def call(
    body, outs, flops, *args, scratch=(), spaces=None, out_spaces=None, aliases=None, vmem=40
):
    spaces = spaces or [pltpu.VMEM] * len(args)
    out_spaces = out_spaces or [pltpu.VMEM] * len(outs)
    moved = sum(a.size * a.dtype.itemsize for a in args) + sum(
        o.size * o.dtype.itemsize for o in outs
    )
    return pl.pallas_call(
        body,
        out_shape=outs,
        in_specs=[pl.BlockSpec(memory_space=space) for space in spaces],
        out_specs=[pl.BlockSpec(memory_space=space) for space in out_spaces],
        input_output_aliases=aliases or {},
        scratch_shapes=list(scratch),
        compiler_params=pltpu.CompilerParams(vmem_limit_bytes=vmem * 2**20),
        cost_estimate=pl.CostEstimate(flops=flops, bytes_accessed=moved, transcendentals=0),
        interpret=INTERPRET,
    )(*args)


def silu(v):
    half = 0.5 * v
    return half + half * jnp.tanh(half)


def split(v):
    hi = v.astype(BF16)
    return hi, (v - hi.astype(F32)).astype(BF16)


def iota(shape, dim):
    return lax.broadcasted_iota(jnp.int32, shape, dim)


def as_column(row):
    heads = row.shape[1]
    same = iota((PAD_HEADS, heads), 0) == iota((PAD_HEADS, heads), 1)
    return jnp.sum(jnp.where(same, row, 0.0), axis=1, keepdims=True)


def head_spread(width, dtype):
    return (iota((PAD_HEADS, width), 1) // HEADDIM == iota((PAD_HEADS, width), 0)).astype(dtype)


def spread_tokens(per_head, spread2):
    hi, lo = split(per_head)
    return dot(jnp.concatenate([hi, lo], axis=0), spread2, TN)


def spread_row(column, spread_f32):
    return jnp.sum(spread_f32 * column, axis=0, keepdims=True)


def fetch(sems, *pairs):
    copies = [pltpu.make_async_copy(a, b, sems.at[i]) for i, (a, b) in enumerate(pairs)]
    for copy in copies:
        copy.start()
    return copies


def conv_silu(padded, taps_ref, at, rows):
    first = 8 - (CONV - 1) + at
    total = taps_ref[0:1, :] * padded[first : first + rows, :]
    for k in range(1, CONV):
        total += taps_ref[k : k + 1, :] * padded[first + k : first + k + rows, :]
    return silu(total).astype(BF16)


def front_kernel(
    x_hbm, bc_hbm, dt_hbm, tap_x_hbm, tap_bc_hbm, bias_hbm, alog_hbm,
    xc_ref, bcc_ref, cum_ref, logstep_ref, state_ref, tail_ref,
    x_ref, bc_ref, dt_ref, tap_x_ref, tap_bc_ref, bias_ref, alog_ref,
    x_scr, bc_scr, logit_scr, fed_scr, sems,
):
    copies = fetch(
        sems, (dt_hbm, dt_ref), (bias_hbm, bias_ref), (alog_hbm, alog_ref), (bc_hbm, bc_ref),
        (tap_bc_hbm, tap_bc_ref), (tap_x_hbm, tap_x_ref), (x_hbm, x_ref),
    )
    tokens, width = x_ref.shape
    heads = dt_ref.shape[0]
    for copy in copies[:3]:
        copy.wait()
    logit_scr[...] = jnp.zeros_like(logit_scr)
    logit_scr[0:heads, :] = dt_ref[...].astype(F32)
    logits = logit_scr[...] + as_column(bias_ref[...])
    small = jnp.exp(-jnp.abs(logits))
    series = small * (1.0 - small * (0.5 - small * (1.0 / 3.0 - small * 0.25)))
    step = jnp.maximum(logits, 0.0) + jnp.where(small < 0.015625, series, jnp.log(1.0 + small))
    logstep = jnp.log(step)
    rate = -jnp.exp(as_column(alog_ref[...])) * step
    upto = (iota((CHUNK, CHUNK), 0) <= iota((CHUNK, CHUNK), 1)).astype(F32)
    run = jnp.zeros((PAD_HEADS, 1), F32)
    sums = []
    for at in range(0, tokens, CHUNK):
        within = dot(rate[:, at : at + CHUNK], upto, precision=HIGH) + run
        run = within[:, CHUNK - 1 :]
        sums.append(within)
    cum = jnp.concatenate(sums, axis=1)
    cum_ref[...] = cum
    logstep_ref[...] = logstep
    spread = head_spread(width, BF16)
    tail = spread_tokens(jnp.exp(run - cum + logstep), jnp.concatenate([spread, spread], axis=0))
    tail_ref[...] = tail[:RIM, :]

    for copy in copies[3:]:
        copy.wait()
    bc_scr[0:8, :] = jnp.zeros((8, bc_scr.shape[1]), F32)
    bc_scr[8:, :] = bc_ref[...].astype(F32)
    x_scr[0:8, :] = jnp.zeros((8, width), F32)
    x_scr[8:, :] = x_ref[...].astype(F32)
    for at in range(0, tokens, CHUNK):
        rows = slice(at, at + CHUNK)
        bcc_ref[rows, :] = conv_silu(bc_scr, tap_bc_ref, at, CHUNK)
        xc = conv_silu(x_scr, tap_x_ref, at, CHUNK)
        xc_ref[rows, :] = xc
        fed_scr[rows, :] = (xc.astype(F32) * tail[rows, :]).astype(BF16)
    fed_scr[0:RIM, :] = jnp.zeros((RIM, width), BF16)
    state_ref[...] = dot(bcc_ref[:, :STATE], fed_scr[...], TN)


def pack_decay(total, width):
    spread = head_spread(width, F32)
    hi, lo = split(total)
    even = iota((1, width), 1) % 2 == 0
    return jnp.where(even, spread_row(hi.astype(F32), spread), spread_row(lo.astype(F32), spread))


def rim_kernel(
    rim_ref, x_hbm, bc_hbm, tap_x_hbm, tap_bc_hbm, cum_ref, tail_ref, state_ref,
    xc_ref, bcc_ref, piece_ref, x_ref, bc_ref, tap_x_ref, tap_bc_ref, x_scr, bc_scr, piece_scr, sems,
):
    copies = fetch(
        sems, (x_hbm.at[0:RIM, :], x_ref), (bc_hbm.at[0:RIM, :], bc_ref),
        (tap_x_hbm, tap_x_ref), (tap_bc_hbm, tap_bc_ref),
    )
    width = x_ref.shape[1]
    rim = rim_ref[...].astype(F32)
    x_scr[0:8, :] = rim[RIM - 8 :, :width]
    bc_scr[0:8, :] = rim[RIM - 8 :, width:]
    last = cum_ref.shape[1] - 1
    decay = pack_decay(cum_ref[:, last:], width)
    for copy in copies:
        copy.wait()
    x_scr[8:, :] = x_ref[...].astype(F32)
    bc_scr[8:, :] = bc_ref[...].astype(F32)
    xc = conv_silu(x_scr, tap_x_ref, 0, RIM)
    bcc = conv_silu(bc_scr, tap_bc_ref, 0, RIM)
    xc_ref[...] = xc
    bcc_ref[...] = bcc
    fed = (xc.astype(F32) * tail_ref[...]).astype(BF16)
    state = state_ref[...] + dot(bcc[:, :STATE], fed, TN)
    each = STATE // Z_RING
    blocks = width // LANES
    for j in range(Z_RING):
        for b in range(blocks):
            at = j * PIECE + b * each
            piece_scr[at : at + each, :] = state[
                j * each : (j + 1) * each, b * LANES : (b + 1) * LANES
            ]
        at = j * PIECE + blocks * each
        piece_scr[at : at + 8, :] = jnp.zeros((8, LANES), F32)
        for b in range(blocks):
            piece_scr[at + b : at + b + 1, :] = decay[:, b * LANES : (b + 1) * LANES]
    piece_ref[...] = piece_scr[...].astype(BF16)


def local_kernel(
    xc_ref, xc_rim_ref, bcc_ref, bcc_rim_ref, cum_ref, logstep_ref, z_hbm, skip_hbm,
    own_ref, reach_ref, c_ref, held, xs, bs, z_ref, skip_ref, sems,
):
    copies = fetch(sems, (skip_hbm, skip_ref), (z_hbm, z_ref))
    tokens, width = xc_ref.shape
    xs[...] = xc_ref[...]
    xs[0:RIM, :] = xc_rim_ref[...]
    bs[...] = bcc_ref[...]
    bs[0:RIM, :] = bcc_rim_ref[...]
    c_ref[...] = bs[:, STATE:]
    spread = head_spread(width, BF16)
    spread2 = jnp.concatenate([spread, spread], axis=0)
    spread_f = head_spread(width, F32)
    causal = iota((CHUNK, CHUNK), 0) >= iota((CHUNK, CHUNK), 1)
    left = iota((CHUNK, LANES), 1) < HEADDIM
    held[...] = jnp.zeros_like(held)
    before = jnp.zeros((PAD_HEADS, 1), F32)
    for copy in copies:
        copy.wait()
    skip = spread_row(as_column(skip_ref[...]), spread_f)
    for at in range(0, tokens, CHUNK):
        rows = slice(at, at + CHUNK)
        b_part, c_part = bs[rows, :STATE], bs[rows, STATE:]
        cum = cum_ref[:, rows]
        source = logstep_ref[:, rows] - cum
        cum_cols = cum.T
        last = cum[:, CHUNK - 1 :]
        cb = dot(c_part, b_part, NT)
        gate = silu(z_ref[rows, :].astype(F32))
        reach_ref[rows, :] = spread_tokens(jnp.exp(cum), spread2) * gate
        fresh = spread_tokens(jnp.exp(cum - before), spread2)
        carried = dot(c_part, held[...].astype(BF16)) * fresh
        for pair in range(width // LANES):
            cols = slice(pair * LANES, (pair + 1) * LANES)
            mixes = []
            for head in (2 * pair, 2 * pair + 1):
                power = cum_cols[:, head : head + 1] + source[head : head + 1, :]
                mixes.append((cb * jnp.exp(jnp.where(causal, power, MASKED))).astype(BF16))
            x_part = xs[rows, cols]
            blank = jnp.zeros_like(x_part)
            x_two = jnp.concatenate(
                [jnp.where(left, x_part, blank), jnp.where(left, blank, x_part)], axis=0
            )
            y = dot(jnp.concatenate(mixes, axis=1), x_two) + carried[:, cols]
            y += skip[:, cols] * x_part.astype(F32)
            own_ref[rows, cols] = y * gate[:, cols]
        if at + CHUNK < tokens:
            tail = spread_tokens(jnp.exp(last + source), spread2)
            fed = (xs[rows, :].astype(F32) * tail).astype(BF16)
            kept = spread_row(jnp.exp(last - before), spread_f)
            held[...] = held[...] * kept + dot(b_part, fed, TN)
            before = last


def decay_rows(wide, at):
    both = wide[at : at + 8, :]
    even = iota((8, LANES), 1) % 2 == 0
    return both + jnp.where(even, pltpu.roll(both, LANES - 1, 1), pltpu.roll(both, 1, 1))


def total_kernel(blocks, in_ref, out_ref, wide):
    wide[...] = in_ref[...].astype(F32)
    carry = [jnp.zeros((8, LANES), F32)] * blocks
    passed = jnp.zeros((8, LANES), F32)
    for place in range(Z_RING):
        at = place * PIECE
        logs = decay_rows(wide, at + 8 * blocks)
        passed += logs
        kept = jnp.exp(logs)
        carry = [
            kept[b : b + 1, :] * carry[b] + wide[at + 8 * b : at + 8 * b + 8, :]
            for b in range(blocks)
        ]
    for peer in range(out_ref.shape[0]):
        for b in range(blocks):
            out_ref[peer, 8 * b : 8 * b + 8, :] = carry[b]
        out_ref[peer, 8 * blocks : 8 * blocks + 8, :] = passed


def scan_kernel(blocks, in_ref, total_ref, place_ref, out_ref, wide):
    wide[...] = in_ref[...].astype(F32)
    carry = [jnp.zeros((8, LANES), F32)] * blocks
    for peer in range(total_ref.shape[0] - 1):
        earlier = peer < place_ref[0, 0]
        kept = jnp.exp(total_ref[peer, 8 * blocks : 8 * blocks + 8, :])
        carry = [
            jnp.where(
                earlier,
                kept[b : b + 1, :] * carry[b] + total_ref[peer, 8 * b : 8 * b + 8, :],
                carry[b],
            )
            for b in range(blocks)
        ]
    for place in range(Z_RING):
        at = place * PIECE
        kept = jnp.exp(decay_rows(wide, at + 8 * blocks))
        for b in range(blocks):
            part = wide[at + 8 * b : at + 8 * b + 8, :]
            wide[at + 8 * b : at + 8 * b + 8, :] = carry[b]
            carry[b] = kept[b : b + 1, :] * carry[b] + part
    out_ref[...] = wide[...].astype(BF16)


def rim_source_kernel(x_hbm, bc_hbm, out_ref, sems):
    tokens, width = x_hbm.shape
    for copy in fetch(
        sems,
        (x_hbm.at[tokens - RIM :, :], out_ref.at[:, 0:width]),
        (bc_hbm.at[tokens - RIM :, :], out_ref.at[:, width:]),
    ):
        copy.wait()


def gate_kernel(
    own_ref, reach_ref, c_ref, piece_ref, gain_ref, place_ref, gated_ref, square_ref, wide, state,
):
    tokens, width = own_ref.shape
    blocks = width // LANES
    each = STATE // Z_RING
    wide[...] = piece_ref[...].astype(F32)
    for j in range(Z_RING):
        for b in range(blocks):
            at = j * PIECE + b * each
            state[j * each : (j + 1) * each, b * LANES : (b + 1) * LANES] = wide[at : at + each, :]
    incoming = state[...].astype(BF16)
    ones = jnp.ones((16, 2 * width), BF16)
    totals = []
    for at in range(0, tokens, CHUNK):
        rows = slice(at, at + CHUNK)
        y = own_ref[rows, :] + reach_ref[rows, :] * dot(c_ref[rows, :], incoming)
        gated_ref[rows, :] = (y * gain_ref[...]).astype(BF16)
        hi, lo = split(y * y)
        totals.append(dot(ones, jnp.concatenate([hi, lo], axis=1), NT))
    hi, lo = split(jnp.concatenate(totals, axis=1))
    row = iota((16, tokens), 0)
    mine = 2 * place_ref[0, 1]
    zero = jnp.zeros((16, tokens), F32)
    square_ref[...] = jnp.where(
        row == mine, hi.astype(F32), jnp.where(row == mine + 1, lo.astype(F32), zero)
    ).astype(BF16)


def project_half(
    gated_hbm, w_hbm, place_ref, half, out_hbm, gated, w_ref, acc, stage, sems, out_sems, gap
):
    span = w_ref.shape[0]
    parts = sems.shape[0] - 1
    step = span // parts
    copies = fetch(
        sems,
        (gated_hbm, gated),
        *[
            (
                w_hbm.at[pl.ds(pl.multiple_of(half * span + k * step, step), step), :],
                w_ref.at[k * step : (k + 1) * step, :],
            )
            for k in range(parts)
        ],
    )
    copies[0].wait()
    for k in range(parts):
        rows = slice(k * step, (k + 1) * step)
        copies[1 + k].wait()
        acc[rows, :] = dot(w_ref[rows, :], gated[...], NT)
    blocks = TARGETS // 2
    block = span // blocks
    shard = block // (Z_RING // 2)
    size = block + gap
    sent = []
    for back in range(blocks):
        at = back * size
        stage[at : at + block, :] = jnp.concatenate(
            [
                acc[z * block // 2 + back * shard : z * block // 2 + (back + 1) * shard, :]
                for z in range(Z_RING // 2)
            ],
            axis=0,
        ).astype(BF16)
        to = pl.multiple_of(lax.rem(place_ref[0, 0] + blocks - back, blocks) * size, size)
        copy = pltpu.make_async_copy(
            stage.at[at : at + size, :], out_hbm.at[pl.ds(to, size), :], out_sems.at[back]
        )
        copy.start()
        sent.append(copy)
    for copy in sent:
        copy.wait()


def given_kernel(
    gated_hbm, square_ref, w_hbm, place_ref, out_hbm, gated, w_ref, acc, stage, sems, out_sems
):
    size = stage.shape[0] // (TARGETS // 2)
    for x in range(TARGETS // 2):
        stage[(x + 1) * size - 16 : (x + 1) * size, :] = square_ref[...]
    half = 1 - lax.rem(place_ref[0, 1], 2)
    project_half(
        gated_hbm, w_hbm, place_ref, half, out_hbm, gated, w_ref, acc, stage, sems, out_sems, 16
    )


def kept_kernel(gated_hbm, w_hbm, place_ref, out_hbm, gated, w_ref, acc, stage, sems, out_sems):
    half = lax.rem(place_ref[0, 1], 2)
    project_half(
        gated_hbm, w_hbm, place_ref, half, out_hbm, gated, w_ref, acc, stage, sems, out_sems, 0
    )


def pair_kernel(kept_ref, got_ref, square_ref, out_ref):
    block = kept_ref.shape[0] // (TARGETS // 2)
    for y in range(TARGETS // 2):
        to = y * (block + 16)
        rows = slice(to, to + block)
        out_ref[rows, :] = (
            kept_ref[y * block : (y + 1) * block, :].astype(F32) + got_ref[rows, :].astype(F32)
        ).astype(BF16)
        rows = slice(to + block, to + block + 16)
        out_ref[rows, :] = (square_ref[...].astype(F32) + got_ref[rows, :].astype(F32)).astype(BF16)


def scale_kernel(in_ref, out_ref):
    block = out_ref.shape[0]
    parts = TARGETS // 2
    each = block + 16
    total = jnp.zeros((1, out_ref.shape[1]), F32)
    for y in range(parts):
        part = in_ref[y * each + block : (y + 1) * each, :].astype(F32)
        total += jnp.sum(part, axis=0, keepdims=True)
    scale = lax.rsqrt(total / CHANNELS + EPSILON)
    mixed = in_ref[0:block, :].astype(F32)
    for y in range(1, parts):
        mixed += in_ref[y * each : y * each + block, :].astype(F32)
    out_ref[...] = (mixed * scale).astype(BF16)


def shaped(shape, dtype):
    return jax.ShapeDtypeStruct(shape, dtype)


def held_like(*arrays):
    return tuple(pltpu.VMEM(a.shape, a.dtype) for a in arrays)


def front(x_in, bc_in, dt_t, conv_x, conv_bc, dt_bias, a_log):
    tokens, width = x_in.shape
    args = (x_in, bc_in, dt_t, conv_x, conv_bc, dt_bias, a_log)
    return call(
        front_kernel,
        [
            shaped((tokens, width), BF16),
            shaped((tokens, 2 * STATE), BF16),
            shaped((PAD_HEADS, tokens), F32),
            shaped((PAD_HEADS, tokens), F32),
            shaped((STATE, width), F32),
            shaped((RIM, width), F32),
        ],
        8 * tokens * width * STATE,
        *args,
        spaces=[pltpu.HBM] * 7,
        vmem=FULL,
        scratch=held_like(*args)
        + (
            pltpu.VMEM((tokens + 8, width), F32),
            pltpu.VMEM((tokens + 8, 2 * STATE), F32),
            pltpu.VMEM((PAD_HEADS, tokens), F32),
            pltpu.VMEM((tokens, width), BF16),
            pltpu.SemaphoreType.DMA((7,)),
        ),
    )


def add_rim(rim, x_in, bc_in, conv_x, conv_bc, cum, tail, state):
    width = x_in.shape[1]
    return call(
        rim_kernel,
        [
            shaped((RIM, width), BF16),
            shaped((RIM, 2 * STATE), BF16),
            shaped((Z_RING * PIECE, LANES), BF16),
        ],
        2 * 128 * width * STATE,
        rim, x_in, bc_in, conv_x, conv_bc, cum, tail, state,
        spaces=[pltpu.VMEM] + [pltpu.HBM] * 4 + [pltpu.VMEM] * 3,
        vmem=FULL,
        scratch=(
            pltpu.VMEM((RIM, width), BF16),
            pltpu.VMEM((RIM, 2 * STATE), BF16),
            *held_like(conv_x, conv_bc),
            pltpu.VMEM((RIM + 8, width), F32),
            pltpu.VMEM((RIM + 8, 2 * STATE), F32),
            pltpu.VMEM((Z_RING * PIECE, LANES), F32),
            pltpu.SemaphoreType.DMA((4,)),
        ),
    )


def local(xc, xc_rim, bcc, bcc_rim, cum, logstep, z_gate, d_skip):
    tokens, width = xc.shape
    return call(
        local_kernel,
        [shaped((tokens, width), F32)] * 2 + [shaped((tokens, STATE), BF16)],
        12 * tokens * width * STATE,
        xc, xc_rim, bcc, bcc_rim, cum, logstep, z_gate, d_skip,
        spaces=[pltpu.VMEM] * 6 + [pltpu.HBM] * 2,
        scratch=(pltpu.VMEM((STATE, width), F32),)
        + held_like(xc, bcc, z_gate, d_skip)
        + (pltpu.SemaphoreType.DMA((2,)),),
    )


def row_total(pieces, width, peers):
    def body(*refs):
        total_kernel(width // LANES, *refs)

    return call(
        body,
        [shaped((peers, PIECE, LANES), F32)],
        pieces.size * 4,
        pieces,
        scratch=(pltpu.VMEM(pieces.shape, F32),),
    )[0]


def scan(pieces, totals, place, width):
    def body(*refs):
        scan_kernel(width // LANES, *refs)

    return call(
        body,
        [shaped(pieces.shape, BF16)],
        pieces.size * 4,
        pieces, totals, place,
        spaces=[pltpu.VMEM, pltpu.VMEM, pltpu.SMEM],
        scratch=(pltpu.VMEM(pieces.shape, F32),),
    )[0]


def rim_source(x_in, bc_in):
    return call(
        rim_source_kernel,
        [shaped((RIM, x_in.shape[1] + bc_in.shape[1]), BF16)],
        0,
        x_in, bc_in,
        spaces=[pltpu.HBM] * 2,
        vmem=FULL,
        scratch=(pltpu.SemaphoreType.DMA((2,)),),
    )[0]


def gate(own, reach, c_part, pieces, norm_gain, place):
    tokens, width = own.shape
    return call(
        gate_kernel,
        [shaped((tokens, width), BF16), shaped((16, tokens), BF16)],
        2 * tokens * width * STATE,
        own, reach, c_part, pieces, norm_gain[None], place,
        spaces=[pltpu.VMEM] * 5 + [pltpu.SMEM],
        scratch=(pltpu.VMEM(pieces.shape, F32), pltpu.VMEM((STATE, width), F32)),
    )


def half_scratch(gated, weight, rows):
    columns, width = weight.shape
    tokens = gated.shape[0]
    return (
        *held_like(gated),
        pltpu.VMEM((columns // 2, width), BF16),
        pltpu.VMEM((columns // 2, tokens), F32),
        pltpu.VMEM((rows, tokens), BF16),
        pltpu.SemaphoreType.DMA((3,)),
        pltpu.SemaphoreType.DMA((TARGETS // 2,)),
    )


def given_part(gated, squares, weight, place):
    tokens, width = gated.shape
    half = weight.shape[0] // 2
    rows = half + TARGETS // 2 * 16
    return call(
        given_kernel,
        [shaped((rows, tokens), BF16)],
        2 * tokens * width * half,
        gated, squares, weight, place,
        spaces=[pltpu.HBM, pltpu.VMEM, pltpu.HBM, pltpu.SMEM],
        out_spaces=[pltpu.HBM],
        vmem=FULL - 2,
        scratch=half_scratch(gated, weight, rows),
    )[0]


def kept_part(gated, weight, place):
    tokens, width = gated.shape
    half = weight.shape[0] // 2
    return call(
        kept_kernel,
        [shaped((half, tokens), BF16)],
        2 * tokens * width * half,
        gated, weight, place,
        spaces=[pltpu.HBM, pltpu.HBM, pltpu.SMEM],
        out_spaces=[pltpu.HBM],
        vmem=FULL - 2,
        scratch=half_scratch(gated, weight, half),
    )[0]


def pair_sum(kept, got, squares):
    return call(pair_kernel, [shaped(got.shape, BF16)], got.size, kept, got, squares)[0]


def scaled(parts):
    rows, tokens = parts.shape
    block = rows // (TARGETS // 2) - 16
    return call(scale_kernel, [shaped((block, tokens), BF16)], rows * tokens, parts)[0]


def on_device(
    x_in, bc_in, z_gate, dt_in, conv_x, conv_bc, dt_bias, a_log, d_skip, norm_gain, out_weight
):
    tokens, width = x_in.shape
    count = lax.axis_size("seq")
    rows = count // Z_RING
    along_z = [[x * Z_RING + z for z in range(Z_RING)] for x in range(rows)]
    along_x = [[x * Z_RING + z for x in range(rows)] for z in range(Z_RING)]
    weight = jnp.concatenate(
        [out_weight.T]
        + [
            lax.ppermute(
                out_weight.T, "seq", [(i, (i + back * Z_RING) % count) for i in range(count)]
            )
            for back in range(1, rows)
        ],
        axis=0,
    )
    weight = lax.all_gather(weight, "seq", axis=0, tiled=True, axis_index_groups=along_z)
    rim = lax.ppermute(rim_source(x_in, bc_in), "seq", [(i, i + 1) for i in range(count - 1)])
    place = jnp.stack(
        [lax.axis_index("seq") // Z_RING, lax.axis_index("tp")]
    ).astype(jnp.int32)[None]

    xc, bcc, cum, logstep, state, tail = front(
        x_in, bc_in, dt_in.T, conv_x, conv_bc, dt_bias[None], a_log[None]
    )
    xc_rim, bcc_rim, pieces = add_rim(rim, x_in, bc_in, conv_x, conv_bc, cum, tail, state)
    pieces = lax.all_to_all(pieces, "seq", 0, 0, tiled=True, axis_index_groups=along_z)
    own, reach, c_part = local(xc, xc_rim, bcc, bcc_rim, cum, logstep, z_gate, d_skip[None])
    totals = row_total(pieces, width, rows)
    totals = lax.all_to_all(totals, "seq", 0, 0, tiled=True, axis_index_groups=along_x)
    pieces = scan(pieces, totals, place, width)
    pieces = lax.all_to_all(pieces, "seq", 0, 0, tiled=True, axis_index_groups=along_z)

    gated, squares = gate(own, reach, c_part, pieces, norm_gain, place)
    given = given_part(gated, squares, weight, place)
    got = lax.ppermute(given, "tp", [(i, i ^ 1) for i in range(TARGETS)])
    kept = kept_part(gated, weight, place)
    parts = pair_sum(kept, got, squares)
    along_y = [[core + 2 * y for y in range(TARGETS // 2)] for core in range(2)]
    parts = lax.all_to_all(parts, "tp", 0, 0, tiled=True, axis_index_groups=along_y)
    return scaled(parts).T


def solution(mesh):
    in_specs = (
        P("seq", "tp"),
        P("seq", None),
        P("seq", "tp"),
        P("seq", "tp"),
        P(None, "tp"),
        P(),
        P("tp"),
        P("tp"),
        P("tp"),
        P("tp"),
        P("tp", "seq"),
    )
    return jax.shard_map(
        on_device, mesh=mesh, in_specs=in_specs, out_specs=P("seq", "tp"), check_vma=False
    )
```

```python
import jax
import jax.numpy as jnp
from jax import lax
from jax.experimental import pallas as pl
from jax.experimental.pallas import tpu as pltpu
from jax.sharding import PartitionSpec as P

CHANNELS = 5120
HEADDIM = 64
STATE = 128
CONV = 4
CHUNK = 128
LANES = 128
RIM = 16
PAD_HEADS = 16
Z_RING = 16
PIECE = 48
TARGETS = 8
FULL = 63
EPSILON = 1e-05
HIGH = lax.Precision.HIGHEST
F32 = jnp.float32
BF16 = jnp.bfloat16
MASKED = -1e30
INTERPRET = False

NT = (((1,), (1,)), ((), ()))
TN = (((0,), (0,)), ((), ()))
NN = (((1,), (0,)), ((), ()))


def dot(a, b, dims=NN, precision=None):
    return lax.dot_general(a, b, dims, precision=precision, preferred_element_type=F32)


def call(
    body, outs, flops, *args, scratch=(), spaces=None, out_spaces=None, aliases=None, vmem=40
):
    spaces = spaces or [pltpu.VMEM] * len(args)
    out_spaces = out_spaces or [pltpu.VMEM] * len(outs)
    moved = sum(a.size * a.dtype.itemsize for a in args) + sum(
        o.size * o.dtype.itemsize for o in outs
    )
    return pl.pallas_call(
        body,
        out_shape=outs,
        in_specs=[pl.BlockSpec(memory_space=space) for space in spaces],
        out_specs=[pl.BlockSpec(memory_space=space) for space in out_spaces],
        input_output_aliases=aliases or {},
        scratch_shapes=list(scratch),
        compiler_params=pltpu.CompilerParams(vmem_limit_bytes=vmem * 2**20),
        cost_estimate=pl.CostEstimate(flops=flops, bytes_accessed=moved, transcendentals=0),
        interpret=INTERPRET,
    )(*args)


def silu(v):
    half = 0.5 * v
    return half + half * jnp.tanh(half)


def split(v):
    hi = v.astype(BF16)
    return hi, (v - hi.astype(F32)).astype(BF16)


def iota(shape, dim):
    return lax.broadcasted_iota(jnp.int32, shape, dim)


def as_column(row):
    heads = row.shape[1]
    same = iota((PAD_HEADS, heads), 0) == iota((PAD_HEADS, heads), 1)
    return jnp.sum(jnp.where(same, row, 0.0), axis=1, keepdims=True)


def head_spread(width, dtype):
    return (iota((PAD_HEADS, width), 1) // HEADDIM == iota((PAD_HEADS, width), 0)).astype(dtype)


def spread_tokens(per_head, spread2):
    hi, lo = split(per_head)
    return dot(jnp.concatenate([hi, lo], axis=0), spread2, TN)


def spread_row(column, spread_f32):
    return jnp.sum(spread_f32 * column, axis=0, keepdims=True)


def fetch(sems, *pairs):
    copies = [pltpu.make_async_copy(a, b, sems.at[i]) for i, (a, b) in enumerate(pairs)]
    for copy in copies:
        copy.start()
    return copies


def conv_silu(padded, taps_ref, at, rows):
    first = 8 - (CONV - 1) + at
    total = taps_ref[0:1, :] * padded[first : first + rows, :]
    for k in range(1, CONV):
        total += taps_ref[k : k + 1, :] * padded[first + k : first + k + rows, :]
    return silu(total).astype(BF16)


def front_kernel(
    x_hbm, bc_hbm, dt_hbm, tap_x_hbm, tap_bc_hbm, bias_hbm, alog_hbm,
    xc_ref, bcc_ref, cum_ref, logstep_ref, state_ref, tail_ref,
    x_ref, bc_ref, dt_ref, tap_x_ref, tap_bc_ref, bias_ref, alog_ref,
    x_scr, bc_scr, logit_scr, fed_scr, sems,
):
    copies = fetch(
        sems, (dt_hbm, dt_ref), (bias_hbm, bias_ref), (alog_hbm, alog_ref), (bc_hbm, bc_ref),
        (tap_bc_hbm, tap_bc_ref), (tap_x_hbm, tap_x_ref), (x_hbm, x_ref),
    )
    tokens, width = x_ref.shape
    heads = dt_ref.shape[0]
    for copy in copies[:3]:
        copy.wait()
    logit_scr[...] = jnp.zeros_like(logit_scr)
    logit_scr[0:heads, :] = dt_ref[...].astype(F32)
    logits = logit_scr[...] + as_column(bias_ref[...])
    small = jnp.exp(-jnp.abs(logits))
    series = small * (1.0 - small * (0.5 - small * (1.0 / 3.0 - small * 0.25)))
    step = jnp.maximum(logits, 0.0) + jnp.where(small < 0.015625, series, jnp.log(1.0 + small))
    logstep = jnp.log(step)
    rate = -jnp.exp(as_column(alog_ref[...])) * step
    upto = (iota((CHUNK, CHUNK), 0) <= iota((CHUNK, CHUNK), 1)).astype(F32)
    run = jnp.zeros((PAD_HEADS, 1), F32)
    sums = []
    for at in range(0, tokens, CHUNK):
        within = dot(rate[:, at : at + CHUNK], upto, precision=HIGH) + run
        run = within[:, CHUNK - 1 :]
        sums.append(within)
    cum = jnp.concatenate(sums, axis=1)
    cum_ref[...] = cum
    logstep_ref[...] = logstep
    spread = head_spread(width, BF16)
    tail = spread_tokens(jnp.exp(run - cum + logstep), jnp.concatenate([spread, spread], axis=0))
    tail_ref[...] = tail[:RIM, :]

    for copy in copies[3:]:
        copy.wait()
    bc_scr[0:8, :] = jnp.zeros((8, bc_scr.shape[1]), F32)
    bc_scr[8:, :] = bc_ref[...].astype(F32)
    x_scr[0:8, :] = jnp.zeros((8, width), F32)
    x_scr[8:, :] = x_ref[...].astype(F32)
    for at in range(0, tokens, CHUNK):
        rows = slice(at, at + CHUNK)
        bcc_ref[rows, :] = conv_silu(bc_scr, tap_bc_ref, at, CHUNK)
        xc = conv_silu(x_scr, tap_x_ref, at, CHUNK)
        xc_ref[rows, :] = xc
        fed_scr[rows, :] = (xc.astype(F32) * tail[rows, :]).astype(BF16)
    fed_scr[0:RIM, :] = jnp.zeros((RIM, width), BF16)
    state_ref[...] = dot(bcc_ref[:, :STATE], fed_scr[...], TN)


def pack_decay(total, width):
    spread = head_spread(width, F32)
    hi, lo = split(total)
    even = iota((1, width), 1) % 2 == 0
    return jnp.where(even, spread_row(hi.astype(F32), spread), spread_row(lo.astype(F32), spread))


def rim_kernel(
    rim_ref, x_hbm, bc_hbm, tap_x_hbm, tap_bc_hbm, cum_ref, tail_ref, state_ref,
    xc_ref, bcc_ref, piece_ref, x_ref, bc_ref, tap_x_ref, tap_bc_ref, x_scr, bc_scr, piece_scr, sems,
):
    copies = fetch(
        sems, (x_hbm.at[0:RIM, :], x_ref), (bc_hbm.at[0:RIM, :], bc_ref),
        (tap_x_hbm, tap_x_ref), (tap_bc_hbm, tap_bc_ref),
    )
    width = x_ref.shape[1]
    rim = rim_ref[...].astype(F32)
    x_scr[0:8, :] = rim[RIM - 8 :, :width]
    bc_scr[0:8, :] = rim[RIM - 8 :, width:]
    last = cum_ref.shape[1] - 1
    decay = pack_decay(cum_ref[:, last:], width)
    for copy in copies:
        copy.wait()
    x_scr[8:, :] = x_ref[...].astype(F32)
    bc_scr[8:, :] = bc_ref[...].astype(F32)
    xc = conv_silu(x_scr, tap_x_ref, 0, RIM)
    bcc = conv_silu(bc_scr, tap_bc_ref, 0, RIM)
    xc_ref[...] = xc
    bcc_ref[...] = bcc
    fed = (xc.astype(F32) * tail_ref[...]).astype(BF16)
    state = state_ref[...] + dot(bcc[:, :STATE], fed, TN)
    each = STATE // Z_RING
    blocks = width // LANES
    for j in range(Z_RING):
        for b in range(blocks):
            at = j * PIECE + b * each
            piece_scr[at : at + each, :] = state[
                j * each : (j + 1) * each, b * LANES : (b + 1) * LANES
            ]
        at = j * PIECE + blocks * each
        piece_scr[at : at + 8, :] = jnp.zeros((8, LANES), F32)
        for b in range(blocks):
            piece_scr[at + b : at + b + 1, :] = decay[:, b * LANES : (b + 1) * LANES]
    piece_ref[...] = piece_scr[...].astype(BF16)


def local_kernel(
    xc_ref, xc_rim_ref, bcc_ref, bcc_rim_ref, cum_ref, logstep_ref, z_hbm, skip_hbm,
    own_ref, reach_ref, c_ref, held, xs, bs, z_ref, skip_ref, sems,
):
    copies = fetch(sems, (skip_hbm, skip_ref), (z_hbm, z_ref))
    tokens, width = xc_ref.shape
    xs[...] = xc_ref[...]
    xs[0:RIM, :] = xc_rim_ref[...]
    bs[...] = bcc_ref[...]
    bs[0:RIM, :] = bcc_rim_ref[...]
    c_ref[...] = bs[:, STATE:]
    spread = head_spread(width, BF16)
    spread2 = jnp.concatenate([spread, spread], axis=0)
    spread_f = head_spread(width, F32)
    causal = iota((CHUNK, CHUNK), 0) >= iota((CHUNK, CHUNK), 1)
    left = iota((CHUNK, LANES), 1) < HEADDIM
    held[...] = jnp.zeros_like(held)
    before = jnp.zeros((PAD_HEADS, 1), F32)
    for copy in copies:
        copy.wait()
    skip = spread_row(as_column(skip_ref[...]), spread_f)
    for at in range(0, tokens, CHUNK):
        rows = slice(at, at + CHUNK)
        b_part, c_part = bs[rows, :STATE], bs[rows, STATE:]
        cum = cum_ref[:, rows]
        source = logstep_ref[:, rows] - cum
        cum_cols = cum.T
        last = cum[:, CHUNK - 1 :]
        cb = dot(c_part, b_part, NT)
        gate = silu(z_ref[rows, :].astype(F32))
        reach_ref[rows, :] = spread_tokens(jnp.exp(cum), spread2) * gate
        fresh = spread_tokens(jnp.exp(cum - before), spread2)
        carried = dot(c_part, held[...].astype(BF16)) * fresh
        for pair in range(width // LANES):
            cols = slice(pair * LANES, (pair + 1) * LANES)
            mixes = []
            for head in (2 * pair, 2 * pair + 1):
                power = cum_cols[:, head : head + 1] + source[head : head + 1, :]
                mixes.append((cb * jnp.exp(jnp.where(causal, power, MASKED))).astype(BF16))
            x_part = xs[rows, cols]
            blank = jnp.zeros_like(x_part)
            x_two = jnp.concatenate(
                [jnp.where(left, x_part, blank), jnp.where(left, blank, x_part)], axis=0
            )
            y = dot(jnp.concatenate(mixes, axis=1), x_two) + carried[:, cols]
            y += skip[:, cols] * x_part.astype(F32)
            own_ref[rows, cols] = y * gate[:, cols]
        if at + CHUNK < tokens:
            tail = spread_tokens(jnp.exp(last + source), spread2)
            fed = (xs[rows, :].astype(F32) * tail).astype(BF16)
            kept = spread_row(jnp.exp(last - before), spread_f)
            held[...] = held[...] * kept + dot(b_part, fed, TN)
            before = last


def decay_rows(wide, at):
    both = wide[at : at + 8, :]
    even = iota((8, LANES), 1) % 2 == 0
    return both + jnp.where(even, pltpu.roll(both, LANES - 1, 1), pltpu.roll(both, 1, 1))


def total_kernel(blocks, in_ref, out_ref, wide):
    wide[...] = in_ref[...].astype(F32)
    carry = [jnp.zeros((8, LANES), F32)] * blocks
    passed = jnp.zeros((8, LANES), F32)
    for place in range(Z_RING):
        at = place * PIECE
        logs = decay_rows(wide, at + 8 * blocks)
        passed += logs
        kept = jnp.exp(logs)
        carry = [
            kept[b : b + 1, :] * carry[b] + wide[at + 8 * b : at + 8 * b + 8, :]
            for b in range(blocks)
        ]
    for peer in range(out_ref.shape[0]):
        for b in range(blocks):
            out_ref[peer, 8 * b : 8 * b + 8, :] = carry[b]
        out_ref[peer, 8 * blocks : 8 * blocks + 8, :] = passed


def scan_kernel(blocks, in_ref, total_ref, place_ref, out_ref, wide):
    wide[...] = in_ref[...].astype(F32)
    carry = [jnp.zeros((8, LANES), F32)] * blocks
    for peer in range(total_ref.shape[0] - 1):
        earlier = peer < place_ref[0, 0]
        kept = jnp.exp(total_ref[peer, 8 * blocks : 8 * blocks + 8, :])
        carry = [
            jnp.where(
                earlier,
                kept[b : b + 1, :] * carry[b] + total_ref[peer, 8 * b : 8 * b + 8, :],
                carry[b],
            )
            for b in range(blocks)
        ]
    for place in range(Z_RING):
        at = place * PIECE
        kept = jnp.exp(decay_rows(wide, at + 8 * blocks))
        for b in range(blocks):
            part = wide[at + 8 * b : at + 8 * b + 8, :]
            wide[at + 8 * b : at + 8 * b + 8, :] = carry[b]
            carry[b] = kept[b : b + 1, :] * carry[b] + part
    out_ref[...] = wide[...].astype(BF16)


def rim_source_kernel(x_hbm, bc_hbm, out_ref, sems):
    tokens, width = x_hbm.shape
    for copy in fetch(
        sems,
        (x_hbm.at[tokens - RIM :, :], out_ref.at[:, 0:width]),
        (bc_hbm.at[tokens - RIM :, :], out_ref.at[:, width:]),
    ):
        copy.wait()


def gate_kernel(
    own_ref, reach_ref, c_ref, piece_ref, gain_ref, place_ref, gated_ref, square_ref, wide, state,
):
    tokens, width = own_ref.shape
    blocks = width // LANES
    each = STATE // Z_RING
    wide[...] = piece_ref[...].astype(F32)
    for j in range(Z_RING):
        for b in range(blocks):
            at = j * PIECE + b * each
            state[j * each : (j + 1) * each, b * LANES : (b + 1) * LANES] = wide[at : at + each, :]
    incoming = state[...].astype(BF16)
    ones = jnp.ones((16, 2 * width), BF16)
    totals = []
    for at in range(0, tokens, CHUNK):
        rows = slice(at, at + CHUNK)
        y = own_ref[rows, :] + reach_ref[rows, :] * dot(c_ref[rows, :], incoming)
        gated_ref[:, rows] = (y * gain_ref[...]).T.astype(BF16)
        hi, lo = split(y * y)
        totals.append(dot(ones, jnp.concatenate([hi, lo], axis=1), NT))
    hi, lo = split(jnp.concatenate(totals, axis=1))
    row = iota((16, tokens), 0)
    mine = 2 * place_ref[0, 1]
    zero = jnp.zeros((16, tokens), F32)
    square_ref[...] = jnp.where(
        row == mine, hi.astype(F32), jnp.where(row == mine + 1, lo.astype(F32), zero)
    ).astype(BF16)


def project_half(
    gated_hbm, w_hbm, half, out_hbm, gated, w_ref, acc, stage, sems, out_sems, gap
):
    span = w_ref.shape[0]
    parts = sems.shape[0] - 1
    step = span // parts
    copies = fetch(
        sems,
        (gated_hbm, gated),
        *[
            (
                w_hbm.at[pl.ds(pl.multiple_of(half * span + k * step, step), step), :],
                w_ref.at[k * step : (k + 1) * step, :],
            )
            for k in range(parts)
        ],
    )
    copies[0].wait()
    for k in range(parts):
        rows = slice(k * step, (k + 1) * step)
        copies[1 + k].wait()
        acc[rows, :] = dot(w_ref[rows, :], gated[...])
    blocks = TARGETS // 2
    block = span // blocks
    shard = block // (Z_RING // 2)
    size = block + gap
    sent = []
    for x in range(blocks):
        at = x * size
        stage[at : at + block, :] = jnp.concatenate(
            [
                acc[z * block // 2 + x * shard : z * block // 2 + (x + 1) * shard, :]
                for z in range(Z_RING // 2)
            ],
            axis=0,
        ).astype(BF16)
        part = slice(at, at + size)
        copy = pltpu.make_async_copy(stage.at[part, :], out_hbm.at[part, :], out_sems.at[x])
        copy.start()
        sent.append(copy)
    for copy in sent:
        copy.wait()


def given_kernel(
    gated_hbm, square_ref, w_hbm, place_ref, out_hbm, gated, w_ref, acc, stage, sems, out_sems
):
    size = stage.shape[0] // (TARGETS // 2)
    for x in range(TARGETS // 2):
        stage[(x + 1) * size - 16 : (x + 1) * size, :] = square_ref[...]
    half = 1 - lax.rem(place_ref[0, 1], 2)
    project_half(
        gated_hbm, w_hbm, half, out_hbm, gated, w_ref, acc, stage, sems, out_sems, 16
    )


def kept_kernel(gated_hbm, w_hbm, place_ref, out_hbm, gated, w_ref, acc, stage, sems, out_sems):
    half = lax.rem(place_ref[0, 1], 2)
    project_half(
        gated_hbm, w_hbm, half, out_hbm, gated, w_ref, acc, stage, sems, out_sems, 0
    )


def pair_kernel(kept_ref, got_ref, square_ref, out_ref):
    block = kept_ref.shape[0] // (TARGETS // 2)
    for y in range(TARGETS // 2):
        to = y * (block + 16)
        rows = slice(to, to + block)
        out_ref[rows, :] = (
            kept_ref[y * block : (y + 1) * block, :].astype(F32) + got_ref[rows, :].astype(F32)
        ).astype(BF16)
        rows = slice(to + block, to + block + 16)
        out_ref[rows, :] = (square_ref[...].astype(F32) + got_ref[rows, :].astype(F32)).astype(BF16)


def scale_kernel(in_ref, out_ref):
    block = out_ref.shape[0]
    parts = TARGETS // 2
    each = block + 16
    total = jnp.zeros((1, out_ref.shape[1]), F32)
    for y in range(parts):
        part = in_ref[y * each + block : (y + 1) * each, :].astype(F32)
        total += jnp.sum(part, axis=0, keepdims=True)
    scale = lax.rsqrt(total / CHANNELS + EPSILON)
    mixed = in_ref[0:block, :].astype(F32)
    for y in range(1, parts):
        mixed += in_ref[y * each : y * each + block, :].astype(F32)
    out_ref[...] = (mixed * scale).astype(BF16)


def shaped(shape, dtype):
    return jax.ShapeDtypeStruct(shape, dtype)


def held_like(*arrays):
    return tuple(pltpu.VMEM(a.shape, a.dtype) for a in arrays)


def front(x_in, bc_in, dt_t, conv_x, conv_bc, dt_bias, a_log):
    tokens, width = x_in.shape
    args = (x_in, bc_in, dt_t, conv_x, conv_bc, dt_bias, a_log)
    return call(
        front_kernel,
        [
            shaped((tokens, width), BF16),
            shaped((tokens, 2 * STATE), BF16),
            shaped((PAD_HEADS, tokens), F32),
            shaped((PAD_HEADS, tokens), F32),
            shaped((STATE, width), F32),
            shaped((RIM, width), F32),
        ],
        8 * tokens * width * STATE,
        *args,
        spaces=[pltpu.HBM] * 7,
        vmem=FULL,
        scratch=held_like(*args)
        + (
            pltpu.VMEM((tokens + 8, width), F32),
            pltpu.VMEM((tokens + 8, 2 * STATE), F32),
            pltpu.VMEM((PAD_HEADS, tokens), F32),
            pltpu.VMEM((tokens, width), BF16),
            pltpu.SemaphoreType.DMA((7,)),
        ),
    )


def add_rim(rim, x_in, bc_in, conv_x, conv_bc, cum, tail, state):
    width = x_in.shape[1]
    return call(
        rim_kernel,
        [
            shaped((RIM, width), BF16),
            shaped((RIM, 2 * STATE), BF16),
            shaped((Z_RING * PIECE, LANES), BF16),
        ],
        2 * 128 * width * STATE,
        rim, x_in, bc_in, conv_x, conv_bc, cum, tail, state,
        spaces=[pltpu.VMEM] + [pltpu.HBM] * 4 + [pltpu.VMEM] * 3,
        vmem=FULL,
        scratch=(
            pltpu.VMEM((RIM, width), BF16),
            pltpu.VMEM((RIM, 2 * STATE), BF16),
            *held_like(conv_x, conv_bc),
            pltpu.VMEM((RIM + 8, width), F32),
            pltpu.VMEM((RIM + 8, 2 * STATE), F32),
            pltpu.VMEM((Z_RING * PIECE, LANES), F32),
            pltpu.SemaphoreType.DMA((4,)),
        ),
    )


def local(xc, xc_rim, bcc, bcc_rim, cum, logstep, z_gate, d_skip):
    tokens, width = xc.shape
    return call(
        local_kernel,
        [shaped((tokens, width), F32)] * 2 + [shaped((tokens, STATE), BF16)],
        12 * tokens * width * STATE,
        xc, xc_rim, bcc, bcc_rim, cum, logstep, z_gate, d_skip,
        spaces=[pltpu.VMEM] * 6 + [pltpu.HBM] * 2,
        scratch=(pltpu.VMEM((STATE, width), F32),)
        + held_like(xc, bcc, z_gate, d_skip)
        + (pltpu.SemaphoreType.DMA((2,)),),
    )


def row_total(pieces, width, peers):
    def body(*refs):
        total_kernel(width // LANES, *refs)

    return call(
        body,
        [shaped((peers, PIECE, LANES), F32)],
        pieces.size * 4,
        pieces,
        scratch=(pltpu.VMEM(pieces.shape, F32),),
    )[0]


def scan(pieces, totals, place, width):
    def body(*refs):
        scan_kernel(width // LANES, *refs)

    return call(
        body,
        [shaped(pieces.shape, BF16)],
        pieces.size * 4,
        pieces, totals, place,
        spaces=[pltpu.VMEM, pltpu.VMEM, pltpu.SMEM],
        scratch=(pltpu.VMEM(pieces.shape, F32),),
    )[0]


def rim_source(x_in, bc_in):
    return call(
        rim_source_kernel,
        [shaped((RIM, x_in.shape[1] + bc_in.shape[1]), BF16)],
        0,
        x_in, bc_in,
        spaces=[pltpu.HBM] * 2,
        vmem=FULL,
        scratch=(pltpu.SemaphoreType.DMA((2,)),),
    )[0]


def gate(own, reach, c_part, pieces, norm_gain, place):
    tokens, width = own.shape
    return call(
        gate_kernel,
        [shaped((width, tokens), BF16), shaped((16, tokens), BF16)],
        2 * tokens * width * STATE,
        own, reach, c_part, pieces, norm_gain[None], place,
        spaces=[pltpu.VMEM] * 5 + [pltpu.SMEM],
        scratch=(pltpu.VMEM(pieces.shape, F32), pltpu.VMEM((STATE, width), F32)),
    )


def half_scratch(gated, weight, rows):
    columns, width = weight.shape
    tokens = gated.shape[1]
    return (
        *held_like(gated),
        pltpu.VMEM((columns // 2, width), BF16),
        pltpu.VMEM((columns // 2, tokens), F32),
        pltpu.VMEM((rows, tokens), BF16),
        pltpu.SemaphoreType.DMA((3,)),
        pltpu.SemaphoreType.DMA((TARGETS // 2,)),
    )


def given_part(gated, squares, weight, place):
    width, tokens = gated.shape
    half = weight.shape[0] // 2
    rows = half + TARGETS // 2 * 16
    return call(
        given_kernel,
        [shaped((rows, tokens), BF16)],
        2 * tokens * width * half,
        gated, squares, weight, place,
        spaces=[pltpu.HBM, pltpu.VMEM, pltpu.HBM, pltpu.SMEM],
        out_spaces=[pltpu.HBM],
        vmem=FULL - 2,
        scratch=half_scratch(gated, weight, rows),
    )[0]


def kept_part(gated, weight, place):
    width, tokens = gated.shape
    half = weight.shape[0] // 2
    return call(
        kept_kernel,
        [shaped((half, tokens), BF16)],
        2 * tokens * width * half,
        gated, weight, place,
        spaces=[pltpu.HBM, pltpu.HBM, pltpu.SMEM],
        out_spaces=[pltpu.HBM],
        vmem=FULL - 2,
        scratch=half_scratch(gated, weight, half),
    )[0]


def pair_sum(kept, got, squares):
    return call(pair_kernel, [shaped(got.shape, BF16)], got.size, kept, got, squares)[0]


def scaled(parts):
    rows, tokens = parts.shape
    block = rows // (TARGETS // 2) - 16
    return call(scale_kernel, [shaped((block, tokens), BF16)], rows * tokens, parts)[0]


def on_device(
    x_in, bc_in, z_gate, dt_in, conv_x, conv_bc, dt_bias, a_log, d_skip, norm_gain, out_weight
):
    tokens, width = x_in.shape
    count = lax.axis_size("seq")
    rows = count // Z_RING
    along_z = [[x * Z_RING + z for z in range(Z_RING)] for x in range(rows)]
    along_x = [[x * Z_RING + z for x in range(rows)] for z in range(Z_RING)]
    weight = out_weight.T
    for groups in (along_x, along_z):
        weight = lax.all_gather(weight, "seq", axis=0, tiled=True, axis_index_groups=groups)
    rim = lax.ppermute(rim_source(x_in, bc_in), "seq", [(i, i + 1) for i in range(count - 1)])
    place = jnp.stack(
        [lax.axis_index("seq") // Z_RING, lax.axis_index("tp")]
    ).astype(jnp.int32)[None]

    xc, bcc, cum, logstep, state, tail = front(
        x_in, bc_in, dt_in.T, conv_x, conv_bc, dt_bias[None], a_log[None]
    )
    xc_rim, bcc_rim, pieces = add_rim(rim, x_in, bc_in, conv_x, conv_bc, cum, tail, state)
    pieces = lax.all_to_all(pieces, "seq", 0, 0, tiled=True, axis_index_groups=along_z)
    own, reach, c_part = local(xc, xc_rim, bcc, bcc_rim, cum, logstep, z_gate, d_skip[None])
    totals = row_total(pieces, width, rows)
    totals = lax.all_to_all(totals, "seq", 0, 0, tiled=True, axis_index_groups=along_x)
    pieces = scan(pieces, totals, place, width)
    pieces = lax.all_to_all(pieces, "seq", 0, 0, tiled=True, axis_index_groups=along_z)

    gated, squares = gate(own, reach, c_part, pieces, norm_gain, place)
    given = given_part(gated, squares, weight, place)
    got = lax.ppermute(given, "tp", [(i, i ^ 1) for i in range(TARGETS)])
    kept = kept_part(gated, weight, place)
    parts = pair_sum(kept, got, squares)
    along_y = [[core + 2 * y for y in range(TARGETS // 2)] for core in range(2)]
    parts = lax.all_to_all(parts, "tp", 0, 0, tiled=True, axis_index_groups=along_y)
    return scaled(parts).T


def solution(mesh):
    in_specs = (
        P("seq", "tp"),
        P("seq", None),
        P("seq", "tp"),
        P("seq", "tp"),
        P(None, "tp"),
        P(),
        P("tp"),
        P("tp"),
        P("tp"),
        P("tp"),
        P("tp", "seq"),
    )
    return jax.shard_map(
        on_device, mesh=mesh, in_specs=in_specs, out_specs=P("seq", "tp"), check_vma=False
    )
```
